32 devices in a mesh: fsdp: 32 (over z, y, x, core).
Axes of the slice: x: 2, y: 2, z: 4, core: 2. Of those that a mesh axis runs over, the one named last changes fastest.
Arguments:
- images: bfloat16 [256, 197, 768], P('fsdp'), may hold values from -6 to 6
- counts: int32 [32], P('fsdp'), may hold values from 1 to 8, as said below
- norm1_gain: bfloat16 [768], P('fsdp'), may hold values from 0.25 to 1.75
- norm1_bias: bfloat16 [768], P('fsdp'), may hold values from -4 to 4
- w_qkv: bfloat16 [768, 2304], P('fsdp'), may hold values from -0.21875 to 0.21875
- q_bias: bfloat16 [768], P('fsdp'), may hold values from -4 to 4
- v_bias: bfloat16 [768], P('fsdp'), may hold values from -4 to 4
- w_out: bfloat16 [768, 768], P('fsdp'), may hold values from -1.25 to 1.25
- out_bias: bfloat16 [768], P('fsdp'), may hold values from -4 to 4
- norm2_gain: bfloat16 [768], P('fsdp'), may hold values from 0.25 to 1.75
- norm2_bias: bfloat16 [768], P('fsdp'), may hold values from -4 to 4
- w_up: bfloat16 [768, 3072], P('fsdp'), may hold values from -0.21875 to 0.21875
- up_bias: bfloat16 [3072], P('fsdp'), may hold values from -4 to 4
- w_down: bfloat16 [3072, 768], P('fsdp'), may hold values from -0.15625 to 0.15625
- down_bias: bfloat16 [768], P('fsdp'), may hold values from -4 to 4
- cotangent: bfloat16 [256, 197, 768], P('fsdp'), may hold values from -6 to 6
Outputs:
- output: bfloat16 [256, 197, 768], P('fsdp')
- grad_images: float32 [256, 197, 768], P('fsdp')
- grad_norm1_gain: float32 [768], P('fsdp')
- grad_norm1_bias: float32 [768], P('fsdp')
- grad_w_qkv: float32 [768, 2304], P('fsdp')
- grad_q_bias: float32 [768], P('fsdp')
- grad_v_bias: float32 [768], P('fsdp')
- grad_w_out: float32 [768, 768], P('fsdp')
- grad_out_bias: float32 [768], P('fsdp')
- grad_norm2_gain: float32 [768], P('fsdp')
- grad_norm2_bias: float32 [768], P('fsdp')
- grad_w_up: float32 [768, 3072], P('fsdp')
- grad_up_bias: float32 [3072], P('fsdp')
- grad_w_down: float32 [3072, 768], P('fsdp')
- grad_down_bias: float32 [768], P('fsdp')
The draws below stay inside these ranges and needn't reach their ends.
Inputs may be any that keep to these rules, and one draw needn't show every extreme that they name: `counts`: number of live image slots on each device; slots below it hold images, the rest are empty. Some device holds 8.
All inputs are finite; a program needn't handle non-finite values.
Results may differ from the reference program's by a relative error of at most 0.013.
Values may be sent and summed in bfloat16 or wider, within the bound.
No kernel may reach another device: no remote copies, remote signals or barrier semaphores. Data moves between devices by JAX's collectives and lax.ppermute only.
A program may use at most 256 MiB of HBM per device.

```python
import jax
import jax.numpy as jnp
from jax import lax

D = 768
H = 12
HD = 64
FF = 3072
L = 197
CAP = 8
IMAGES = 256
N_FSDP = 32


def draw_counts(key, part):
    key = jax.random.fold_in(key, 7)
    key_counts, key_fullest = jax.random.split(key)
    drawn_counts = jax.random.randint(key_counts, (N_FSDP,), 1, CAP + 1)
    fullest = jax.random.randint(key_fullest, (), 0, N_FSDP)
    positions = jnp.arange(N_FSDP, dtype=jnp.int32)
    return jnp.where(positions == fullest, CAP, drawn_counts).astype(jnp.int32)


def level_of(own_key, shape, cuts, low, largest):
    level = 1.0
    for axis_at, shards_of in cuts:
        steps = jax.random.uniform(jax.random.fold_in(jax.random.fold_in(own_key, 6), axis_at), (shards_of,), jnp.float32, low / len(cuts), largest / len(cuts))
        level = level * jnp.repeat(jnp.exp(steps), shape[axis_at] // shards_of).reshape((-1,) + (1,) * (len(shape) - 1 - axis_at))
    return level


def bell_draw(own_key, shape, spread, reach, cuts=(), kind=jnp.bfloat16):
    loudness = level_of(own_key, shape, cuts, -0.22, 0.18) if cuts else 1.0
    array = jax.random.normal(own_key, shape, jnp.float32) * spread * loudness
    return jnp.minimum(jnp.maximum(array, -reach), reach).astype(kind)


def setup_inputs(seed: int = 0) -> dict:
    key_list = jax.random.split(jax.random.key(seed), 17)
    images = bell_draw(key_list[0], (IMAGES, L, D), 1.0, 6.0, ((0, 32),))
    counts = draw_counts(jax.random.fold_in(key_list[16], 71), 0)
    norm1_gain = jnp.clip(1.0 + 0.15 * jax.random.normal(key_list[2], (D,), jnp.float32), 0.25, 1.75).astype(jnp.bfloat16)
    norm1_bias = bell_draw(key_list[3], (D,), 0.3, 4.0, ((0, 32),))
    w_qkv = bell_draw(key_list[4], (D, 3 * D), D ** -0.5, 0.21875, ((0, 32),))
    q_bias = bell_draw(key_list[5], (D,), 0.5, 4.0, ((0, 32),))
    v_bias = bell_draw(key_list[6], (D,), 0.5, 4.0, ((0, 32),))
    w_out = bell_draw(key_list[7], (D, D), (D // 32) ** -0.5, 1.25, ((0, 32),))
    out_bias = bell_draw(key_list[8], (D,), 0.3, 4.0, ((0, 32),))
    norm2_gain = jnp.clip(1.0 + 0.15 * jax.random.normal(key_list[9], (D,), jnp.float32), 0.25, 1.75).astype(jnp.bfloat16)
    norm2_bias = bell_draw(key_list[10], (D,), 0.3, 4.0, ((0, 32),))
    w_up = bell_draw(key_list[11], (D, FF), D ** -0.5, 0.21875, ((0, 32),))
    up_bias = bell_draw(key_list[12], (FF,), 0.5, 4.0, ((0, 32),))
    w_down = bell_draw(key_list[13], (FF, D), (FF // 2) ** -0.5, 0.15625, ((0, 32),))
    down_bias = bell_draw(key_list[14], (D,), 0.3, 4.0, ((0, 32),))
    cotangent = bell_draw(key_list[15], (IMAGES, L, D), 1.0, 6.0, ((0, 32),))
    return dict(images=images, counts=counts, norm1_gain=norm1_gain, norm1_bias=norm1_bias, w_qkv=w_qkv, q_bias=q_bias, v_bias=v_bias, w_out=w_out, out_bias=out_bias, norm2_gain=norm2_gain, norm2_bias=norm2_bias, w_up=w_up, up_bias=up_bias, w_down=w_down, down_bias=down_bias, cotangent=cotangent)


epsilon = 1e-06
highest = lax.Precision.HIGHEST

@jax.custom_vjp
def low(v):
    return lax.optimization_barrier(v.astype(jnp.bfloat16)).astype(jnp.float32)

@jax.custom_vjp
def low_back(v):
    return v

def low_keep(v):
    return (low(v), None)

def low_pass(kept, grad):
    return (grad,)

def back_keep(v):
    return (v, None)

def back_low(kept, grad):
    return (low(grad),)
low.defvjp(low_keep, low_pass)
low_back.defvjp(back_keep, back_low)

def layer_norm(matrix, scale_vec, shift_vec):
    centred = matrix - lax.optimization_barrier(jnp.mean(matrix, axis=-1, keepdims=True))
    scaled = centred * lax.rsqrt(lax.optimization_barrier(jnp.mean(centred * centred, axis=-1, keepdims=True)) + epsilon)
    return scaled * scale_vec + shift_vec

def matmul(left_side, right_side):
    return jnp.dot(left_side, right_side, precision=highest)

def encoder_block(image_slab, live_mask, params):
    norm1_gain, norm1_bias, w_qkv, q_bias, v_bias, w_out, out_bias, norm2_gain, norm2_bias, w_up, up_bias, w_down, down_bias = params
    flat_rows = image_slab.reshape(CAP * L, D)
    normed_one = low(layer_norm(flat_rows, norm1_gain, norm1_bias))
    projected = matmul(normed_one, w_qkv)
    query_rows = low(low_back(projected[:, :D] + q_bias)).reshape(CAP, L, H, HD)
    key_rows = low(low_back(projected[:, D:2 * D])).reshape(CAP, L, H, HD)
    value_rows = low(low_back(projected[:, 2 * D:] + v_bias)).reshape(CAP, L, H, HD)
    scores = jnp.einsum('bqhe,bkhe->bhqk', query_rows, key_rows, precision=highest) * HD ** (-0.5)
    scores = low_back(scores)
    soft_weights = low(jax.nn.softmax(scores, axis=-1))
    attended = jnp.einsum('bhqk,bkhe->bqhe', soft_weights, value_rows, precision=highest).reshape(CAP * L, D)
    attended = low(low_back(attended))
    residual = flat_rows + low_back(matmul(attended, w_out) + out_bias)
    normed_two = low(layer_norm(residual, norm2_gain, norm2_bias))
    hidden_pre = low_back(matmul(normed_two, w_up) + up_bias)
    hidden_act = low(jax.nn.gelu(hidden_pre, approximate=False))
    branch_mlp = low_back(matmul(hidden_act, w_down) + down_bias)
    return live_mask * (residual + branch_mlp).reshape(CAP, L, D)

def reference(images, counts, norm1_gain, norm1_bias, w_qkv, q_bias, v_bias, w_out, out_bias, norm2_gain, norm2_bias, w_up, up_bias, w_down, down_bias, cotangent):
    params = tuple((member.astype(jnp.float32) for member in (norm1_gain, norm1_bias, w_qkv, q_bias, v_bias, w_out, out_bias, norm2_gain, norm2_bias, w_up, up_bias, w_down, down_bias)))
    groups = images.astype(jnp.float32).reshape(N_FSDP, CAP, L, D)
    slot_ids = jnp.arange(CAP, dtype=jnp.int32)
    live = (slot_ids[None, :] < counts.astype(jnp.int32)[:, None]).astype(jnp.float32)[:, :, None, None]

    def forward(slabs, weights):

        def one_group(bundle):
            return encoder_block(bundle[0], bundle[1], weights)
        return lax.map(jax.checkpoint(one_group), (slabs, live))
    result, pullback = jax.vjp(forward, groups, params)
    grad_groups, grads = pullback(cotangent.astype(jnp.float32).reshape(N_FSDP, CAP, L, D))
    return (result.reshape(IMAGES, L, D).astype(jnp.bfloat16), grad_groups.reshape(IMAGES, L, D), grads[0], grads[1], grads[2], grads[3], grads[4], grads[5], grads[6], grads[7], grads[8], grads[9], grads[10], grads[11], grads[12])
```

```python
import functools

import jax
import jax.numpy as jnp
from jax import lax
from jax.experimental import pallas as pl
from jax.experimental.pallas import tpu as pltpu
from jax.sharding import PartitionSpec as P

D = 768
H = 12
HD = 64
L = 197
RP = 208
HALF = 3 * D // 2
T = 2
VROWS = 12
GAIN1, SHIFT1, QB, VB, OB, GAIN2, SHIFT2, DB, UB = range(9)

epsilon = 1e-06
half_root = 0.7071067811865476
inv_root_tau = 0.3989422804014327
f32 = jnp.float32
bf16 = jnp.bfloat16
MIB = 1 << 20


def normalize(matrix):
    centred = matrix - jnp.mean(matrix, axis=-1, keepdims=True)
    inverse = lax.rsqrt(jnp.mean(centred * centred, axis=-1, keepdims=True) + epsilon)
    return (centred * inverse, inverse)


def normalize_back(grad_scaled, normed, inverse):
    mean_grad = jnp.mean(grad_scaled, axis=-1, keepdims=True)
    mean_proj = jnp.mean(grad_scaled * normed, axis=-1, keepdims=True)
    return inverse * (grad_scaled - mean_grad - normed * mean_proj)


def dot(a, b):
    return lax.dot_general(a, b, (((1,), (0,)), ((), ())), preferred_element_type=f32)


def dot_nt(a, b):
    return lax.dot_general(a, b, (((1,), (1,)), ((), ())), preferred_element_type=f32)


def dot_tn(a, b):
    return lax.dot_general(a, b, (((0,), (0,)), ((), ())), preferred_element_type=f32)


def rows_of(ref):
    block = ref[...].astype(f32)
    row = lax.broadcasted_iota(jnp.int32, block.shape, 1)
    return jnp.where(row < L, block, 0.0).reshape(block.shape[0] * RP, D)


def forward_attention(x_ref, vec_ref, wa_ref, wb_ref, a1_ref, qkv_ref, o_ref, lse_ref):
    vec = vec_ref[...]
    normed, _ = normalize(rows_of(x_ref))
    a = (normed * vec[GAIN1 : GAIN1 + 1] + vec[SHIFT1 : SHIFT1 + 1]).astype(bf16)
    a1_ref[...] = a
    first = dot(a, wa_ref[...])
    qkv_ref[:, :D] = ((first[:, :D] + vec[QB : QB + 1]) * HD**-0.5).astype(bf16)
    qkv_ref[:, D:HALF] = first[:, D:].astype(bf16)
    second = dot(a, wb_ref[...])
    qkv_ref[:, HALF : 2 * D] = second[:, : 2 * D - HALF].astype(bf16)
    qkv_ref[:, 2 * D :] = (second[:, 2 * D - HALF :] + vec[VB : VB + 1]).astype(bf16)
    lane = lax.broadcasted_iota(jnp.int32, (RP, 128), 1)
    key_row = lax.broadcasted_iota(jnp.int32, (RP, RP), 0)

    def pair(step, carry):
        t = step // (H // 2)
        p = step % (H // 2)
        r = pl.ds(pl.multiple_of(t * RP, 16), RP)
        at = lambda k: pl.ds(pl.multiple_of(k * D + p * 128, 128), 128)
        q2 = qkv_ref[r, at(0)]
        k2 = qkv_ref[r, at(1)]
        v2 = qkv_ref[r, at(2)]
        total_t = None
        for hh in range(2):
            own = (lane // HD) == hh
            qh = jnp.where(own, q2, jnp.zeros_like(q2))
            vh = jnp.where(own, v2, jnp.zeros_like(v2))
            s = jnp.where(key_row < L, dot_nt(k2, qh), -1e30)
            top = jnp.max(s, axis=0, keepdims=True)
            e = jnp.exp(s - top)
            total = jnp.sum(e, axis=0, keepdims=True)
            w = (e * (1.0 / total)).astype(bf16)
            lse_ref[t, pl.ds(2 * p + hh, 1), :] = top + jnp.log(total)
            part = dot_tn(vh, w)
            total_t = part if total_t is None else total_t + part
        o_ref[r, at(0)] = total_t.T.astype(bf16)
        return carry

    lax.fori_loop(0, x_ref.shape[0] * (H // 2), pair, 0)


def gelu_parts(z):
    e = jnp.exp(-0.5 * z * z)
    return 0.5 * (1.0 + lax.erf(z * half_root)), e


def middle(
    count_ref, x_ref, c_ref, o_ref, vec_ref, wo_ref, wu_ref, wd_ref,
    out_ref, dr_ref, do_ref, gwo_ref, gwu_ref, gwd_ref, gvec_ref,
    acc_o, acc_u, acc_d, stage, sems,
):
    step = pl.program_id(0)
    images = x_ref.shape[0]

    @pl.when(step == 0)
    def _():
        acc_o[...] = jnp.zeros_like(acc_o)
        acc_u[...] = jnp.zeros_like(acc_u)
        acc_d[...] = jnp.zeros_like(acc_d)
        gvec_ref[...] = jnp.zeros_like(gvec_ref)

    vec = vec_ref[...]
    row = lambda k: vec[k : k + 1]
    shape = (images, RP, D)
    slot = lax.broadcasted_iota(jnp.int32, shape, 0) + step * images
    live = (slot < count_ref[0]).reshape(images * RP, D)
    c = jnp.where(live, rows_of(c_ref), 0.0)
    cb = c.astype(bf16)
    o = o_ref[...]
    r = rows_of(x_ref) + dot(o, wo_ref[...]) + row(OB)
    n2, i2 = normalize(r)
    a2 = (n2 * row(GAIN2) + row(SHIFT2)).astype(bf16)
    a2t = a2.T
    gvec_ref[DB : DB + 1] += jnp.sum(c, axis=0, keepdims=True)

    def chunk(j, carry):
        y, da2 = carry
        cols = pl.ds(pl.multiple_of(j * D, D), D)
        wu = wu_ref[:, cols]
        wd = wd_ref[cols, :]
        z = dot(a2, wu) + vec_ref[pl.ds(UB + j, 1), :]
        phi, e = gelu_parts(z)
        u = (z * phi).astype(bf16)
        dz = (dot_nt(cb, wd) * (phi + z * e * inv_root_tau)).astype(bf16)
        acc_d[cols, :] += dot_tn(u, cb)
        acc_u[:, cols] += dot(a2t, dz)
        gvec_ref[pl.ds(UB + j, 1), :] += jnp.sum(dz.astype(f32), axis=0, keepdims=True)
        return y + dot(u, wd), da2 + dot_nt(dz, wu)

    zero = jnp.zeros((images * RP, D), f32)
    y, da2 = lax.fori_loop(0, wd_ref.shape[0] // D, chunk, (zero, zero))
    out = jnp.where(live, r + y + row(DB), 0.0)
    out_ref[...] = out.reshape(shape).astype(bf16)
    gvec_ref[GAIN2 : GAIN2 + 1] += jnp.sum(da2 * n2, axis=0, keepdims=True)
    gvec_ref[SHIFT2 : SHIFT2 + 1] += jnp.sum(da2, axis=0, keepdims=True)
    dr = c + normalize_back(da2 * row(GAIN2), n2, i2)
    dr_ref[...] = dr
    drb = dr.astype(bf16)
    gvec_ref[OB : OB + 1] += jnp.sum(drb.astype(f32), axis=0, keepdims=True)
    acc_o[...] += dot_tn(o, drb)
    do_ref[...] = dot_nt(drb, wo_ref[...]).astype(bf16)

    @pl.when(step == pl.num_programs(0) - 1)
    def _():
        at = [pl.ds(j * D, D) for j in range(wd_ref.shape[0] // D)]
        parts = [(acc_u.at[:, k], gwu_ref.at[:, k]) for k in at]
        parts += [(acc_d.at[k], gwd_ref.at[k]) for k in at]
        parts += [(acc_o, gwo_ref)]
        copies = []
        for k, (source, target) in enumerate(parts):
            if k >= 2:
                copies[k - 2].wait()
            stage[k % 2] = source[...].astype(bf16)
            copies.append(pltpu.make_async_copy(stage.at[k % 2], target, sems.at[k % 2]))
            copies[k].start()
        copies[-2].wait()
        copies[-1].wait()


def backward_attention(qkv_ref, lse_ref, do_ref, a1_ref, dp_ref, gwa_ref, gwb_ref, gvec_ref, acc):
    step = pl.program_id(0)
    images = lse_ref.shape[0]

    @pl.when(step == 0)
    def _():
        acc[...] = jnp.zeros_like(acc)
        gvec_ref[...] = jnp.zeros_like(gvec_ref)

    lane = lax.broadcasted_iota(jnp.int32, (RP, 128), 1)
    key_row = lax.broadcasted_iota(jnp.int32, (RP, RP), 0)

    def pair(step, carry):
        t = step // (H // 2)
        p = step % (H // 2)
        r = pl.ds(pl.multiple_of(t * RP, 16), RP)
        at = lambda k: pl.ds(pl.multiple_of(k * D + p * 128, 128), 128)
        q2 = qkv_ref[r, at(0)]
        k2 = qkv_ref[r, at(1)]
        v2 = qkv_ref[r, at(2)]
        do2 = do_ref[r, at(0)]
        dv = dk = dqt = None
        for hh in range(2):
            own = (lane // HD) == hh
            zero = jnp.zeros_like(q2)
            qh = jnp.where(own, q2, zero)
            kh = jnp.where(own, k2, zero)
            doh = jnp.where(own, do2, zero)
            s = dot_nt(k2, qh)
            w = jnp.where(key_row < L, jnp.exp(s - lse_ref[t, pl.ds(2 * p + hh, 1), :]), 0.0)
            dw = dot_nt(v2, doh)
            inner = jnp.sum(dw * w, axis=0, keepdims=True)
            ds = (w * (dw - inner)).astype(bf16)
            dv_h = dot(w.astype(bf16), doh)
            dk_h = dot(ds, qh)
            dq_h = dot_tn(kh, ds)
            dv = dv_h if dv is None else dv + dv_h
            dk = dk_h if dk is None else dk + dk_h
            dqt = dq_h if dqt is None else dqt + dq_h
        dp_ref[r, at(0)] = (dqt.T * HD**-0.5).astype(bf16)
        dp_ref[r, at(1)] = dk.astype(bf16)
        dp_ref[r, at(2)] = dv.astype(bf16)
        return carry

    lax.fori_loop(0, images * (H // 2), pair, 0)
    acc[...] += dot_tn(a1_ref[...], dp_ref[...])
    gvec_ref[QB : QB + 1] += jnp.sum(dp_ref[:, :D].astype(f32), axis=0, keepdims=True)
    gvec_ref[VB : VB + 1] += jnp.sum(dp_ref[:, 2 * D :].astype(f32), axis=0, keepdims=True)

    @pl.when(step == pl.num_programs(0) - 1)
    def _():
        gwa_ref[...] = acc[:, :HALF].astype(bf16)
        gwb_ref[...] = acc[:, HALF:].astype(bf16)


def backward_input(x_ref, dp_ref, dr_ref, vec_ref, wa_ref, wb_ref, gi_ref, gvec_ref):
    @pl.when(pl.program_id(0) == 0)
    def _():
        gvec_ref[...] = jnp.zeros_like(gvec_ref)

    gain = vec_ref[...][GAIN1 : GAIN1 + 1]
    n1, i1 = normalize(rows_of(x_ref))
    da1 = dot_nt(dp_ref[:, :HALF], wa_ref[...]) + dot_nt(dp_ref[:, HALF:], wb_ref[...])
    gvec_ref[GAIN1 : GAIN1 + 1] += jnp.sum(da1 * n1, axis=0, keepdims=True)
    gvec_ref[SHIFT1 : SHIFT1 + 1] += jnp.sum(da1, axis=0, keepdims=True)
    gi = dr_ref[...] + normalize_back(da1 * gain, n1, i1)
    gi_ref[...] = gi.reshape(x_ref.shape[0], RP, D)


def image_spec():
    return pl.BlockSpec((T, RP, D), lambda i: (i, 0, 0))


def row_spec(width):
    return pl.BlockSpec((T * RP, width), lambda i: (i, 0))


def whole(shape):
    return pl.BlockSpec(shape, lambda i: (0,) * len(shape), pipeline_mode=pl.Buffered(1))


def shaped(shape, kind):
    return jax.ShapeDtypeStruct(shape, kind)


def params(mib):
    return pltpu.CompilerParams(dimension_semantics=("arbitrary",), vmem_limit_bytes=mib * MIB)


def cost(flops, moved, ex=0):
    return pl.CostEstimate(flops=int(flops), bytes_accessed=int(moved), transcendentals=int(ex))


def permute(a, bit, n):
    return lax.ppermute(a, "fsdp", [(i, i ^ bit) for i in range(n)])


def bits_of(n):
    return [1 << k for k in range(n.bit_length() - 1)]


def gather_order(n, swap):
    bits = bits_of(n)
    middle_bits = bits[1:3][::-1] if swap else bits[1:3]
    return bits[3:][::-1] + middle_bits + bits[:1]


def gather(shard, n, me, swap):
    have = []
    a = shard
    for b in gather_order(n, swap):
        got = permute(a, b, n)
        upper = (me & b) != 0
        axis = sum(h > b for h in have)
        a = jnp.stack([jnp.where(upper, got, a), jnp.where(upper, a, got)], axis=axis)
        have.append(b)
    return a.reshape(n * shard.shape[0], shard.shape[1])


def scatter_sum(whole_grad, n, me, swap):
    rows, width = whole_grad.shape
    left = bits_of(n)[::-1]
    a = whole_grad.reshape([2] * len(left) + [rows // n, width])
    for b in gather_order(n, swap)[::-1]:
        axis = left.index(b)
        low = lax.index_in_dim(a, 0, axis, keepdims=False)
        high = lax.index_in_dim(a, 1, axis, keepdims=False)
        upper = (me & b) != 0
        got = permute(jnp.where(upper, low, high).astype(bf16), b, n)
        left.remove(b)
        a = jnp.where(upper, high, low).astype(f32) + got.astype(f32)
        if left:
            a = a.astype(bf16)
    return a.reshape(rows // n, width).astype(f32)


def everywhere(a, n):
    for b in bits_of(n)[::-1]:
        a = a + permute(a, b, n)
    return a


def on_device(
    n,
    images,
    counts,
    norm1_gain,
    norm1_bias,
    w_qkv,
    q_bias,
    v_bias,
    w_out,
    out_bias,
    norm2_gain,
    norm2_bias,
    w_up,
    up_bias,
    w_down,
    down_bias,
    cotangent,
):
    me = lax.axis_index("fsdp")
    slots = images.shape[0]
    total = slots * RP
    ff = n * up_bias.shape[0]
    own = norm1_gain.shape[0]
    own_up = up_bias.shape[0]
    up_at = (UB + (me * own_up) // D, (me * own_up) % D)

    packed = jnp.stack(
        [norm1_gain, norm1_bias, q_bias, v_bias, out_bias, norm2_gain, norm2_bias, down_bias]
    )
    vec = jnp.zeros((UB + ff // D, D), bf16)
    vec = lax.dynamic_update_slice(vec, packed, (0, me * own))
    vec = lax.dynamic_update_slice(vec, up_bias[None, :], up_at)
    vec = everywhere(vec, n).astype(f32)
    wa = gather(w_qkv[:, :HALF], n, me, False)
    wb = gather(w_qkv[:, HALF:], n, me, True)
    wo = gather(w_out, n, me, True)
    wu = gather(w_up, n, me, False)
    wd = gather(w_down, n, me, True)

    vspec = whole(vec.shape)
    steps = slots // T
    a1, qkv, o, lse = pl.pallas_call(
        forward_attention,
        grid=(steps,),
        in_specs=[image_spec(), vspec, whole((D, HALF)), whole((D, HALF))],
        out_specs=[row_spec(D), row_spec(3 * D), row_spec(D),
                   pl.BlockSpec((T, H, RP), lambda i: (i, 0, 0))],
        out_shape=[shaped((total, D), bf16), shaped((total, 3 * D), bf16),
                   shaped((total, D), bf16), shaped((slots, H, RP), f32)],
        compiler_params=params(56),
        cost_estimate=cost(total * D * 3 * D * 2 + slots * H * RP * RP * 256 * 4, 20e6, slots * H * RP * RP),
        name="forward_attention",
    )(images, vec, wa, wb)

    out, dr, do, gwo, gwu, gwd, gvec_mid = pl.pallas_call(
        middle,
        grid=(steps,),
        in_specs=[pl.BlockSpec(memory_space=pltpu.SMEM), image_spec(), image_spec(), row_spec(D),
                  vspec, whole((D, D)), whole((D, ff)), whole((ff, D))],
        out_specs=[image_spec(), row_spec(D), row_spec(D)]
        + [pl.BlockSpec(memory_space=pl.ANY)] * 3 + [vspec],
        out_shape=[shaped(images.shape, bf16), shaped((total, D), f32), shaped((total, D), bf16),
                   shaped((D, D), bf16), shaped((D, ff), bf16), shaped((ff, D), bf16),
                   shaped(vec.shape, f32)],
        scratch_shapes=[pltpu.VMEM((D, D), f32), pltpu.VMEM((D, ff), f32), pltpu.VMEM((ff, D), f32),
                        pltpu.VMEM((2, D, D), bf16), pltpu.SemaphoreType.DMA((2,))],
        compiler_params=params(62),
        cost_estimate=cost(total * D * (6 * ff + 3 * D) * 2, 50e6, total * ff),
        name="middle",
    )(counts, images, cotangent, o, vec, wo, wu, wd)

    dp, gwa, gwb, gvec_attn = pl.pallas_call(
        backward_attention,
        grid=(steps,),
        in_specs=[row_spec(3 * D), pl.BlockSpec((T, H, RP), lambda i: (i, 0, 0)), row_spec(D),
                  row_spec(D)],
        out_specs=[row_spec(3 * D), whole((D, HALF)), whole((D, HALF)), vspec],
        out_shape=[shaped((total, 3 * D), bf16), shaped((D, HALF), bf16), shaped((D, HALF), bf16),
                   shaped(vec.shape, f32)],
        scratch_shapes=[pltpu.VMEM((D, 3 * D), f32)],
        compiler_params=params(56),
        cost_estimate=cost(total * D * 3 * D * 2 + slots * H * RP * RP * 256 * 10, 30e6, slots * H * RP * RP),
        name="backward_attention",
    )(qkv, lse, do, a1)

    gi, gvec_in = pl.pallas_call(
        backward_input,
        grid=(steps,),
        in_specs=[image_spec(), row_spec(3 * D), row_spec(D), vspec, whole((D, HALF)),
                  whole((D, HALF))],
        out_specs=[image_spec(), vspec],
        out_shape=[shaped(images.shape, f32), shaped(vec.shape, f32)],
        compiler_params=params(56),
        cost_estimate=cost(total * D * 3 * D * 2, 25e6),
        name="backward_input",
    )(images, dp, dr, vec, wa, wb)

    shard_up = scatter_sum(gwu, n, me, False)
    shard_down = scatter_sum(gwd, n, me, True)
    shard_out = scatter_sum(gwo, n, me, True)
    shard_qkv = jnp.concatenate(
        [scatter_sum(gwa, n, me, False), scatter_sum(gwb, n, me, True)], axis=1
    )
    gvec = everywhere(gvec_mid + gvec_attn + gvec_in, n)
    small = lax.dynamic_slice(gvec, (0, me * own), (UB, own))
    shard_up_shift = lax.dynamic_slice(gvec, up_at, (1, own_up))[0]
    return (
        out,
        gi,
        small[GAIN1],
        small[SHIFT1],
        shard_qkv,
        small[QB],
        small[VB],
        shard_out,
        small[OB],
        small[GAIN2],
        small[SHIFT2],
        shard_up,
        shard_up_shift,
        shard_down,
        small[DB],
    )


def solution(mesh):
    rows = P("fsdp", None)
    cube = P("fsdp", None, None)
    one = P("fsdp")
    return jax.shard_map(
        functools.partial(on_device, mesh.shape["fsdp"]),
        mesh=mesh,
        in_specs=(cube, one, one, one, rows, one, one, rows, one, one, one, rows, one, rows, one, cube),
        out_specs=(cube, cube, one, one, rows, one, one, rows, one, one, one, rows, one, rows, one),
        check_vma=False,
    )
```

```python
import functools

import jax
import jax.numpy as jnp
from jax import lax
from jax.experimental import pallas as pl
from jax.experimental.pallas import tpu as pltpu
from jax.sharding import PartitionSpec as P

D = 768
H = 12
HD = 64
L = 197
RP = 208
HALF = 3 * D // 2
WIDE = 3 * D + 128
HB = D // 2
EDGE = L // 8 * 8
T = 2
GAIN1, SHIFT1, QB, VB, OB, GAIN2, SHIFT2, DB, UB = range(9)

epsilon = 1e-06
half_root = 0.7071067811865476
inv_root_tau = 0.3989422804014327
f32 = jnp.float32
bf16 = jnp.bfloat16
MIB = 1 << 20


UNROLL_F = 3
UNROLL_B = 3
TM = 832
SUB = 768


def normalize(matrix):
    centred = matrix - jnp.mean(matrix, axis=-1, keepdims=True)
    inverse = lax.rsqrt(jnp.mean(centred * centred, axis=-1, keepdims=True) + epsilon)
    return (centred * inverse, inverse)


def normalize_back(grad_scaled, normed, inverse):
    mean_grad = jnp.mean(grad_scaled, axis=-1, keepdims=True)
    mean_proj = jnp.mean(grad_scaled * normed, axis=-1, keepdims=True)
    return inverse * (grad_scaled - mean_grad - normed * mean_proj)


def dot(a, b):
    return lax.dot_general(a, b, (((1,), (0,)), ((), ())), preferred_element_type=f32)


def dot_nt(a, b):
    return lax.dot_general(a, b, (((1,), (1,)), ((), ())), preferred_element_type=f32)


def dot_tn(a, b):
    return lax.dot_general(a, b, (((0,), (0,)), ((), ())), preferred_element_type=f32)


def rows_of(ref):
    block = ref[...].astype(f32)
    row = lax.broadcasted_iota(jnp.int32, block.shape, 1)
    return jnp.where(row < L, block, 0.0).reshape(block.shape[0] * RP, D)


def input_projection(x_ref, w_ref, a1_ref, qkv_ref, vec_ref):
    @pl.when(pl.program_id(0) == 0)
    def _():
        vec_ref[...] = w_ref[:, 3 * D :].astype(f32).T[: vec_ref.shape[0]]

    vec = vec_ref[...]
    normed, _ = normalize(rows_of(x_ref))
    a = (normed * vec[GAIN1 : GAIN1 + 1] + vec[SHIFT1 : SHIFT1 + 1]).astype(bf16)
    a1_ref[...] = a
    for h in range(2):
        at = h * HALF
        p = dot(a, w_ref[:, at : at + HALF])
        qb = vec[QB : QB + 1, h * HB : (h + 1) * HB]
        vb = vec[VB : VB + 1, h * HB : (h + 1) * HB]
        qkv_ref[:, at : at + HB] = ((p[:, :HB] + qb) * HD**-0.5).astype(bf16)
        qkv_ref[:, at + HB : at + 2 * HB] = p[:, HB : 2 * HB].astype(bf16)
        qkv_ref[:, at + 2 * HB : at + HALF] = (p[:, 2 * HB :] + vb).astype(bf16)


PAIRS = HB // 128


def place(step):
    t = step // PAIRS
    p = step % PAIRS
    r = pl.ds(pl.multiple_of(t * RP, 16), RP)
    at = lambda k: pl.ds(pl.multiple_of(k * HB + p * 128, 128), 128)
    return t, p, r, at


def forward_attention(qkv_ref, o_ref, lse_ref):
    lane = lax.broadcasted_iota(jnp.int32, (RP, 128), 1)
    key_row = lax.broadcasted_iota(jnp.int32, (RP - EDGE, RP), 0)

    def pair(h, step, carry):
        t, p, r, at = place(step)
        into = pl.ds(pl.multiple_of(h * HB + p * 128, 128), 128)
        at = lambda k: pl.ds(pl.multiple_of(h * HALF + k * HB + p * 128, 128), 128)
        q2 = qkv_ref[r, at(0)]
        k2 = qkv_ref[r, at(1)]
        v2 = qkv_ref[r, at(2)]
        v2t = v2.T
        zero = jnp.zeros_like(k2)
        both = dot_nt(jnp.concatenate([jnp.where(lane < HD, k2, zero), jnp.where(lane < HD, zero, k2)]), q2)
        parts = []
        for hh in range(2):
            s = both[hh * RP : (hh + 1) * RP]
            s = jnp.concatenate([s[:EDGE], jnp.where(key_row < L - EDGE, s[EDGE:], -1e30)], axis=0)
            top = jnp.max(s, axis=0, keepdims=True)
            e = jnp.exp(s - top)
            total = jnp.sum(e, axis=0, keepdims=True)
            w = (e * (1.0 / total)).astype(bf16)
            lse_ref[t, pl.ds(h * (H // 2) + 2 * p + hh, 1), :] = top + jnp.log(total)
            parts.append(dot(v2t[hh * HD : (hh + 1) * HD], w))
        total_t = jnp.concatenate(parts)
        o_ref[r, into] = total_t.T.astype(bf16)
        return carry

    for h in range(2):
        lax.fori_loop(0, lse_ref.shape[0] * PAIRS, functools.partial(pair, h), 0, unroll=UNROLL_F)


def live_rows(count_ref, images):
    shape = (images, RP, D)
    slot = lax.broadcasted_iota(jnp.int32, shape, 0) + pl.program_id(0) * images
    return (slot < count_ref[0]).reshape(images * RP, D)


def output_projection(count_ref, x_ref, c_ref, o_ref, vec_ref, wo_ref, r_ref, a2_ref, cb_ref):
    vec = vec_ref[...]
    live = live_rows(count_ref, x_ref.shape[0])
    cb_ref[...] = jnp.where(live, rows_of(c_ref), 0.0).astype(bf16)
    r = rows_of(x_ref) + vec[OB : OB + 1] + dot(o_ref[...], wo_ref[...])
    r_ref[...] = r
    n2, _ = normalize(r)
    a2_ref[...] = (n2 * vec[GAIN2 : GAIN2 + 1] + vec[SHIFT2 : SHIFT2 + 1]).astype(bf16)


def gelu_parts(z):
    return 0.5 + 0.5 * lax.erf(z * half_root), jnp.exp(z * z * -0.5)


def tiles(rows, body):
    def tile(i, carry):
        body(pl.ds(pl.multiple_of(i * TM, 16), TM))
        return carry

    lax.fori_loop(0, rows // TM, tile, 0)


def hidden(a2_ref, wu_ref, ub_ref, u_ref, slope_ref):
    def body(r):
        a2 = a2_ref[r, :]
        for k in range(D // SUB):
            c = slice(k * SUB, (k + 1) * SUB)
            z = dot(a2, wu_ref[:, c]) + ub_ref[:, c]
            phi, e = gelu_parts(z)
            u_ref[r, c] = (z * phi).astype(bf16)
            slope_ref[r, c] = (phi + z * e * inv_root_tau).astype(bf16)

    tiles(a2_ref.shape[0], body)


def hidden_back(own, cb_ref, packed_ref, u_ref, slope_ref, dz_ref, wd_ref, gwd_ref, gub_ref, cbt):
    if packed_ref.shape == wd_ref.shape:
        wd_ref[...] = packed_ref[...]
    else:
        packed = packed_ref[...].astype(f32)
        parts = [
            packed[d : d + own, k : k + D]
            for d in range(0, packed.shape[0], own) for k in range(0, packed.shape[1], D)
        ]
        wd_ref[...] = jnp.concatenate(parts).astype(bf16)

    @pl.when(pl.program_id(0) == 0)
    def _():
        cbt[...] = cb_ref[...].T

    gub_ref[...] = jnp.zeros_like(gub_ref)

    def body(r):
        dz = (dot_nt(cb_ref[r, :], wd_ref[...]) * slope_ref[r, :].astype(f32)).astype(bf16)
        dz_ref[r, :] = dz
        gub_ref[0] += jnp.sum(dz.astype(f32), axis=0, keepdims=True)

    tiles(cb_ref.shape[0], body)
    gwd_ref[...] = dot(cbt[...], u_ref[...]).T.astype(bf16)


def up_gradient(a2_ref, dz_ref, gwu_ref, a2t):
    @pl.when(pl.program_id(0) == 0)
    def _():
        a2t[...] = a2_ref[...].T

    gwu_ref[...] = dot(a2t[...], dz_ref[...]).astype(bf16)


def middle_back(
    count_ref, r_ref, u_ref, dz_ref, cb_ref, o_ref, vec_ref, wo_ref, wu_ref, wd_ref,
    out_ref, dr_ref, do_ref, gwo_ref, gvec_ref, acc,
):
    step = pl.program_id(0)

    @pl.when(step == 0)
    def _():
        acc[...] = jnp.zeros_like(acc)
        gvec_ref[...] = jnp.zeros_like(gvec_ref)

    vec = vec_ref[...]
    images = out_ref.shape[0]
    live = live_rows(count_ref, images)
    r = r_ref[...]
    out = jnp.where(live, r + dot(u_ref[...], wd_ref[...]) + vec[DB : DB + 1], 0.0)
    out_ref[...] = out.reshape(images, RP, D).astype(bf16)
    n2, i2 = normalize(r)
    da2 = dot_nt(dz_ref[...], wu_ref[...])
    c = cb_ref[...].astype(f32)
    dr = c + normalize_back(da2 * vec[GAIN2 : GAIN2 + 1], n2, i2)
    dr_ref[...] = dr
    drb = dr.astype(bf16)
    for k, m in enumerate((da2 * n2, da2, drb.astype(f32), c)):
        gvec_ref[k : k + 1] += jnp.sum(m, axis=0, keepdims=True)
    acc[...] += dot_tn(o_ref[...], drb)
    do_ref[...] = dot_nt(drb, wo_ref[...]).astype(bf16)

    @pl.when(step == pl.num_programs(0) - 1)
    def _():
        gwo_ref[...] = acc[...].astype(bf16)


def backward_attention(h, qkv_ref, lse_ref, do_ref, a1_ref, *refs):
    dp_ref, gw_ref, gvec_ref, acc = refs[-4:]
    step = pl.program_id(0)
    images = lse_ref.shape[0]

    @pl.when(step == 0)
    def _():
        acc[...] = jnp.zeros_like(acc)
        gvec_ref[...] = jnp.zeros_like(gvec_ref)

    lane = lax.broadcasted_iota(jnp.int32, (RP, 128), 1)
    key_row = lax.broadcasted_iota(jnp.int32, (RP - EDGE, RP), 0)

    def pair(step, carry):
        t, p, r, at = place(step)
        q2 = qkv_ref[r, at(0)]
        k2 = qkv_ref[r, at(1)]
        v2 = qkv_ref[r, at(2)]
        do2 = do_ref[r, at(0)]
        dv = dk = dqt = None
        for hh in range(2):
            own = (lane // HD) == hh
            zero = jnp.zeros_like(q2)
            qh = jnp.where(own, q2, zero)
            kh = jnp.where(own, k2, zero)
            doh = jnp.where(own, do2, zero)
            s = dot_nt(k2, qh)
            s = s - lse_ref[t, pl.ds(h * (H // 2) + 2 * p + hh, 1), :]
            w = jnp.exp(jnp.concatenate([s[:EDGE], jnp.where(key_row < L - EDGE, s[EDGE:], -1e30)], axis=0))
            dw = dot_nt(v2, doh)
            inner = jnp.sum(dw * w, axis=0, keepdims=True)
            ds = (w * (dw - inner)).astype(bf16)
            dv_h = dot(w.astype(bf16), doh)
            dk_h = dot(ds, qh)
            dq_h = dot_tn(kh, ds)
            dv = dv_h if dv is None else dv + dv_h
            dk = dk_h if dk is None else dk + dk_h
            dqt = dq_h if dqt is None else dqt + dq_h
        dp_ref[r, at(0)] = (dqt.T * HD**-0.5).astype(bf16)
        dp_ref[r, at(1)] = dk.astype(bf16)
        dp_ref[r, at(2)] = dv.astype(bf16)
        return carry

    lax.fori_loop(0, images * PAIRS, pair, 0, unroll=UNROLL_B)
    acc[...] += dot_tn(a1_ref[...], dp_ref[...])
    gvec_ref[0:1] += jnp.sum(dp_ref[:, :HB].astype(f32), axis=0, keepdims=True)
    gvec_ref[1:2] += jnp.sum(dp_ref[:, 2 * HB :].astype(f32), axis=0, keepdims=True)

    @pl.when(step == pl.num_programs(0) - 1)
    def _():
        gw_ref[:, :HALF] = acc[...].astype(bf16)
        if gw_ref.shape[1] > HALF:
            gw_ref[:, HALF:] = refs[0][...]


def backward_input(
    x_ref, dpa_ref, dpb_ref, dr_ref, vec_ref, w_ref, mid_ref, ga_ref, gb_ref, gub_ref,
    gi_ref, gvec_ref, acc,
):
    step = pl.program_id(0)

    @pl.when(step == 0)
    def _():
        acc[...] = jnp.zeros_like(acc)
        for k, name in enumerate((GAIN2, SHIFT2, OB, DB)):
            acc[name : name + 1] = mid_ref[k : k + 1]
        for k, name in enumerate((QB, VB)):
            acc[name : name + 1, :HB] = ga_ref[k : k + 1]
            acc[name : name + 1, HB:] = gb_ref[k : k + 1]
        acc[UB : UB + gub_ref.shape[0]] = gub_ref[...]

    gain = vec_ref[...][GAIN1 : GAIN1 + 1]
    n1, i1 = normalize(rows_of(x_ref))
    da1 = dot_nt(dpa_ref[...], w_ref[:, :HALF]) + dot_nt(dpb_ref[...], w_ref[:, HALF : 3 * D])
    acc[GAIN1 : GAIN1 + 1] += jnp.sum(da1 * n1, axis=0, keepdims=True)
    acc[SHIFT1 : SHIFT1 + 1] += jnp.sum(da1, axis=0, keepdims=True)
    gi = dr_ref[...] + normalize_back(da1 * gain, n1, i1)
    gi_ref[...] = gi.reshape(x_ref.shape[0], RP, D)

    @pl.when(step == pl.num_programs(0) - 1)
    def _():
        gvec_ref[...] = acc[...].T


def image_spec():
    return pl.BlockSpec((T, RP, D), lambda i: (i, 0, 0))


def row_spec(width, column=0):
    return pl.BlockSpec((T * RP, width), lambda i: (i, column))


def lse_spec():
    return pl.BlockSpec((T, H, RP), lambda i: (i, 0, 0))


def whole(shape, column=0):
    at = (0,) * (len(shape) - 1) + (column,)
    return pl.BlockSpec(shape, lambda i: at, pipeline_mode=pl.Buffered(1))


def launch(body, steps, ins, outs, scratch, deps, flops, moved, ex, name, mib):
    n_in, n_dep, n_out = len(ins), len(deps), len(outs)

    def kernel(*refs):
        token = refs[n_in + n_dep + n_out]
        token[...] = jnp.zeros_like(token)
        first_out = n_in + n_dep
        body(*refs[:n_in], *refs[first_out : first_out + n_out], *refs[first_out + n_out + 1 :])

    results = pl.pallas_call(
        kernel,
        grid=(steps,),
        in_specs=[spec for _, spec in ins] + [pl.BlockSpec(memory_space=pl.ANY)] * n_dep,
        out_specs=[spec for _, _, spec in outs] + [whole((1, 1))],
        out_shape=[jax.ShapeDtypeStruct(shape, kind) for shape, kind, _ in outs]
        + [jax.ShapeDtypeStruct((1, 1), f32)],
        scratch_shapes=scratch,
        compiler_params=pltpu.CompilerParams(
            dimension_semantics=("arbitrary",), vmem_limit_bytes=mib * MIB
        ),
        cost_estimate=pl.CostEstimate(
            flops=int(flops), bytes_accessed=int(moved), transcendentals=int(ex)
        ),
        name=name,
    )(*[a for a, _ in ins], *deps)
    return results[:-1], results[-1].reshape(())


def joined(token, arrays, passed):
    anywhere = pl.BlockSpec(memory_space=pl.ANY)
    one = pl.BlockSpec((1, 1), lambda: (0, 0))
    count = len(passed)

    def kernel(*refs):
        refs[len(refs) - count - 1][...] = refs[0][...]

    token, *passed = pl.pallas_call(
        kernel,
        in_specs=[one] + [anywhere] * (count + len(arrays)),
        out_specs=[one] + [anywhere] * count,
        out_shape=[jax.ShapeDtypeStruct((1, 1), f32)]
        + [jax.ShapeDtypeStruct(p.shape, p.dtype) for p in passed],
        input_output_aliases={k + 1: k + 1 for k in range(count)},
        name="joined",
    )(token.reshape(1, 1), *passed, *arrays)
    return token.reshape(()), passed


class Links:
    def __init__(self, n, me):
        self.n = n
        self.me = me
        self.plane = max(1, min(4, n // 2))
        self.depth = n // (2 * self.plane)
        self.core = me % 2
        self.chip = me // 2 % self.plane
        self.level = me // (2 * self.plane)

    def send(self, a, bits):
        return lax.ppermute(a, "fsdp", [(i, i ^ bits) for i in range(self.n)])

    def across_core(self, a):
        return self.send(a, 1)

    def across_plane(self, a, k):
        return self.send(a, 2 * k)

    def across_depth(self, a, k):
        return self.send(a, 2 * self.plane * k)

    def relative(self, core, k, z):
        return core + 2 * k + 2 * self.plane * z


def copy_blocks(pairs, buffer, in_sems, out_sems):
    arriving = []
    for i, (source, _) in enumerate(pairs):
        arriving.append(pltpu.make_async_copy(source, buffer.at[i], in_sems.at[i]))
        arriving[i].start()
    leaving = []
    for i, (_, target) in enumerate(pairs):
        arriving[i].wait()
        leaving.append(pltpu.make_async_copy(buffer.at[i], target, out_sems.at[i]))
        leaving[i].start()
    for c in leaving:
        c.wait()


def blocks_kernel(body, me, ins, outs, n, block, name):
    anywhere = pl.BlockSpec(memory_space=pl.ANY)
    return pl.pallas_call(
        body,
        in_specs=[pl.BlockSpec(memory_space=pltpu.SMEM)] + [anywhere] * len(ins),
        out_specs=[anywhere] * len(outs),
        out_shape=outs,
        scratch_shapes=[
            pltpu.VMEM((n,) + block, bf16), pltpu.SemaphoreType.DMA((n,)), pltpu.SemaphoreType.DMA((n,))
        ],
        compiler_params=pltpu.CompilerParams(vmem_limit_bytes=40 * MIB),
        cost_estimate=pl.CostEstimate(flops=0, bytes_accessed=8_000_000, transcendentals=0),
        name=name,
    )(me.reshape(1), *ins)


def gather(links, shard, deps):
    n, plane, depth = links.n, links.plane, links.depth
    a = jnp.stack([shard] + [links.across_depth(shard, z) for z in range(1, depth)])
    parts = [a] + [links.across_plane(a, k) for k in range(1, plane)]
    parts = parts + [links.across_core(a) for a in parts]

    def assemble(me_ref, *refs):
        out = refs[2 * plane + len(deps)]
        me = me_ref[0]
        copy_blocks(
            [
                (refs[core * plane + k].at[z], out.at[me ^ links.relative(core, k, z)])
                for core in range(2) for k in range(plane) for z in range(depth)
            ],
            *refs[2 * plane + len(deps) + 1 :],
        )

    out = jax.ShapeDtypeStruct((n,) + shard.shape, shard.dtype)
    whole_rows = blocks_kernel(
        assemble, links.me, parts + deps, [out], n, shard.shape, "assemble"
    )[0]
    return whole_rows.reshape(-1, shard.shape[1])


def pick(a, index, axis):
    return lax.dynamic_index_in_dim(a, index, axis, keepdims=False)


class Scatter:
    def __init__(self, links, a):
        n, plane, depth = links.n, links.plane, links.depth
        self.links = links
        self.blocks = a.reshape(depth, plane, 2, a.shape[0] // n, a.shape[1])
        self.sent = pick(self.blocks, 1 - links.core, 2)
        self.ready = []

    def cores(self):
        self.got = self.links.across_core(self.sent)

    def cores_done(self, token, beside=None):
        links = self.links
        own = pick(self.blocks, links.core, 2)

        def to_chip(k):
            at = links.chip ^ k
            part = pick(own, at, 1).astype(f32) + pick(self.got, at, 1).astype(f32) + token
            if beside is not None:
                part = jnp.concatenate([part, pick(beside, at, 1)], axis=-1)
            return part.astype(bf16)

        self.ready = [to_chip(k) for k in range(links.plane)]

    def planes(self):
        self.got = self.ready[:1] + [
            self.links.across_plane(a, k) for k, a in enumerate(self.ready) if k
        ]

    def planes_done(self, token):
        links = self.links

        def to_level(j):
            at = links.level ^ j
            return (sum(pick(g, at, 0).astype(f32) for g in self.got) + token).astype(bf16)

        self.ready = [to_level(j) for j in range(links.depth)]

    def depths(self):
        self.got = self.ready[:1] + [
            self.links.across_depth(a, j) for j, a in enumerate(self.ready) if j
        ]

    def depths_done(self, token):
        self.result = sum(g.astype(f32) for g in self.got) + token


def on_device(
    n,
    images,
    counts,
    norm1_gain,
    norm1_bias,
    w_qkv,
    q_bias,
    v_bias,
    w_out,
    out_bias,
    norm2_gain,
    norm2_bias,
    w_up,
    up_bias,
    w_down,
    down_bias,
    cotangent,
):
    links = Links(n, lax.axis_index("fsdp"))
    slots = images.shape[0]
    total = slots * RP
    steps = slots // T
    ff = n * up_bias.shape[0]
    chunks = ff // D
    own = norm1_gain.shape[0]
    own_up = up_bias.shape[0]
    up_rows = own_up // own

    vectors = [norm1_gain, norm1_bias, q_bias, v_bias, out_bias, norm2_gain, norm2_bias, down_bias]
    vectors += [up_bias[k * own : (k + 1) * own] for k in range(up_rows)]
    shape = (len(vectors), own)
    name = lax.broadcasted_iota(jnp.int32, shape, 0)
    columns = jnp.zeros(shape, bf16)
    for k, v in enumerate(vectors):
        columns = jnp.where(name == k, lax.broadcast_in_dim(v, shape, (1,)), columns)
    columns = columns.T
    columns = jnp.pad(columns, ((0, 0), (0, WIDE - 3 * D - columns.shape[1])))
    heads = [w_qkv[:, k * D + h * HB : k * D + (h + 1) * HB] for h in range(2) for k in range(3)]
    w = gather(links, jnp.concatenate(heads + [columns], axis=1), [images, cotangent])
    packed = [w_down[k * own : (k + 1) * own] for k in range(up_rows)] + [w_up, w_out]
    rest = lax.all_gather(jnp.concatenate(packed, axis=1), "fsdp", axis=0, tiled=True)

    (a1, qkv, vec), _ = launch(
        input_projection, steps,
        [(images, image_spec()), (w, whole((D, WIDE)))],
        [((total, D), bf16, row_spec(D)), ((total, 3 * D), bf16, row_spec(3 * D)),
         ((16, D), f32, whole((16, D)))],
        [], [], total * D * 3 * D * 2, 20e6, 0, "input_projection", 60,
    )
    (o, lse), _ = launch(
        forward_attention, steps,
        [(qkv, row_spec(3 * D))],
        [((total, D), bf16, row_spec(D)), ((slots, H, RP), f32, lse_spec())],
        [], [], slots * H * RP * RP * 256 * 4, 11e6, slots * H * RP * RP, "forward_attention", 60,
    )
    counts_spec = pl.BlockSpec(memory_space=pltpu.SMEM)
    (r, a2, cb), _ = launch(
        output_projection, steps,
        [(counts, counts_spec), (images, image_spec()), (cotangent, image_spec()),
         (o, row_spec(D)), (vec, whole((16, D))), (rest, whole((D, D), 2 * chunks))],
        [((total, D), f32, row_spec(D)), ((total, D), bf16, row_spec(D)),
         ((total, D), bf16, row_spec(D))],
        [], [], total * D * D * 2, 20e6, 0, "output_projection", 60,
    )
    up_shift = vec[UB : UB + up_rows].reshape(up_rows, n, own).transpose(1, 0, 2).reshape(1, ff)
    rows = whole((total, D))
    chunk = pl.BlockSpec((total, D), lambda j: (0, j))
    (u, slope), _ = launch(
        hidden, chunks,
        [(a2, rows), (rest, pl.BlockSpec((D, D), lambda j: (0, j + chunks))),
         (up_shift, pl.BlockSpec((1, D), lambda j: (0, j)))],
        [((total, ff), bf16, chunk), ((total, ff), bf16, chunk)],
        [], [], total * D * ff * 2, 28e6, total * ff, "hidden", 60,
    )
    packed_wd = (rest, pl.BlockSpec((D // up_rows, ff), lambda j: (j, 0)))
    if own % 8:
        wd = rest[:, :ff].reshape(n, own, up_rows, D).transpose(0, 2, 1, 3).reshape(ff, D)
        packed_wd = (wd, pl.BlockSpec((D, D), lambda j: (j, 0)))
    (dz, wd, gwd, gub), _ = launch(
        functools.partial(hidden_back, own), chunks,
        [(cb, rows), packed_wd, (u, chunk), (slope, chunk)],
        [((total, ff), bf16, chunk), ((ff, D), bf16, pl.BlockSpec((D, D), lambda j: (j, 0))),
         ((ff, D), bf16, pl.BlockSpec((D, D), lambda j: (j, 0))),
         ((chunks, 1, D), f32, pl.BlockSpec((1, 1, D), lambda j: (j, 0, 0)))],
        [pltpu.VMEM((D, total), bf16)], [], total * D * ff * 4, 42e6, 0, "hidden_back", 60,
    )
    sd = Scatter(links, gwd)
    (gwu,), token = launch(
        up_gradient, chunks,
        [(a2, rows), (dz, chunk)],
        [((D, ff), bf16, pl.BlockSpec((D, D), lambda j: (0, j)))],
        [pltpu.VMEM((D, total), bf16)], sd.ready, total * D * ff * 2, 18e6, 0, "up_gradient", 60,
    )
    sd.cores()
    sd.cores_done(token)
    su = Scatter(links, gwu)

    (out, dr, do, gwo, gvec_mid), token = launch(
        middle_back, steps,
        [(counts, counts_spec), (r, row_spec(D)), (u, row_spec(ff)), (dz, row_spec(ff)),
         (cb, row_spec(D)), (o, row_spec(D)), (vec, whole((16, D))), (rest, whole((D, D), 2 * chunks)),
         (rest, whole((D, ff), 1)), (wd, whole((ff, D)))],
        [(images.shape, bf16, image_spec()), ((total, D), f32, row_spec(D)),
         ((total, D), bf16, row_spec(D)), ((D, D), bf16, whole((D, D))), ((8, D), f32, whole((8, D)))],
        [pltpu.VMEM((D, D), f32)], sd.ready + su.ready, total * D * (ff + D) * 4, 50e6, 0, "middle_back", 60,
    )
    sd.planes()
    su.cores()
    sd.planes_done(token)
    su.cores_done(token)

    def attention_back(h, carried, deps):
        width = HALF + D * len(carried)
        return launch(
            functools.partial(backward_attention, h), steps,
            [(qkv, row_spec(HALF, h)), (lse, lse_spec()), (do, row_spec(HB, h)), (a1, row_spec(D))]
            + [(a, whole((D, D))) for a in carried],
            [((total, HALF), bf16, row_spec(HALF)), ((D, width), bf16, whole((D, width))),
             ((8, HB), f32, whole((8, HB)))],
            [pltpu.VMEM((D, HALF), f32)], deps,
            total * D * HALF * 2 + slots * H * RP * RP * 256 * 5, 14e6, slots * H * RP * RP // 2,
            "backward_attention", 60,
        )

    (dpa, gwa, gvec_a), token = attention_back(0, [gwo], sd.ready + su.ready)
    su.planes()
    sd.depths()
    su.planes_done(token)
    sd.depths_done(token)
    sa = Scatter(links, gwa)
    (dpb, gwb, gvec_b), token = attention_back(1, [], su.ready + sa.ready)
    su.depths()
    sa.cores()
    su.depths_done(token)
    sa.cores_done(token)
    sb = Scatter(links, gwb)
    gub = gub.reshape(n, up_rows, own).transpose(1, 0, 2).reshape(up_rows, D)
    (gi, gvec), token = launch(
        backward_input, steps,
        [(images, image_spec()), (dpa, row_spec(HALF)), (dpb, row_spec(HALF)), (dr, row_spec(D)),
         (vec, whole((16, D))), (w, whole((D, WIDE))), (gvec_mid, whole((8, D))),
         (gvec_a, whole((8, HB))), (gvec_b, whole((8, HB))), (gub, whole((up_rows, D)))],
        [(images.shape, f32, image_spec()), ((D, 128), f32, whole((D, 128)))],
        [pltpu.VMEM((128, D), f32)], sa.ready + sb.ready, total * D * 3 * D * 2, 25e6, 0, "backward_input", 60,
    )
    sa.planes()
    sb.cores()
    token, (out, gi, gvec) = joined(token, sa.got[1:], [out, gi, gvec])
    gvec = gvec.reshape(links.depth, links.plane, 2, own, 128)
    gvec = pick(gvec, links.core, 2) + links.across_core(pick(gvec, 1 - links.core, 2))
    sb.cores_done(token, gvec)
    sb.planes()
    sa.planes_done(token)
    zero = jnp.zeros((), f32)
    sb.planes_done(zero)
    sb.ready = [jnp.concatenate([x, y], axis=-1) for x, y in zip(sa.ready, sb.ready)]
    sb.depths()
    sb.depths_done(zero)
    fa, fb = sb.result[:, : HALF + D], sb.result[:, HALF + D :]
    shard_up, shard_down = su.result, sd.result
    shard_qkv = jnp.concatenate(
        [f[:, k * HB : (k + 1) * HB] for k in range(3) for f in (fa, fb)], axis=1
    )
    shard_out = fa[:, HALF:]
    small = fb[:, HALF : HALF + UB + up_rows].T
    shard_up_shift = small[UB:].reshape(own_up)
    return (
        out,
        gi,
        small[GAIN1],
        small[SHIFT1],
        shard_qkv,
        small[QB],
        small[VB],
        shard_out,
        small[OB],
        small[GAIN2],
        small[SHIFT2],
        shard_up,
        shard_up_shift,
        shard_down,
        small[DB],
    )


def solution(mesh):
    rows = P("fsdp", None)
    cube = P("fsdp", None, None)
    one = P("fsdp")
    return jax.shard_map(
        functools.partial(on_device, mesh.shape["fsdp"]),
        mesh=mesh,
        in_specs=(cube, one, one, one, rows, one, one, rows, one, one, one, rows, one, rows, one, cube),
        out_specs=(cube, cube, one, one, rows, one, one, rows, one, one, one, rows, one, rows, one),
        check_vma=False,
    )
```

```python
import functools

import jax
import jax.numpy as jnp
from jax import lax
from jax.experimental import pallas as pl
from jax.experimental.pallas import tpu as pltpu
from jax.sharding import PartitionSpec as P

D = 768
H = 12
HD = 64
L = 197
RP = 208
HALF = 3 * D // 2
WIDE = 3 * D + 128
HB = D // 2
EDGE = L // 8 * 8
T = 2
GAIN1, SHIFT1, QB, VB, OB, GAIN2, SHIFT2, DB, UB = range(9)

epsilon = 1e-06
half_root = 0.7071067811865476
inv_root_tau = 0.3989422804014327
f32 = jnp.float32
bf16 = jnp.bfloat16
MIB = 1 << 20


UNROLL_F = 6
UNROLL_B = 6
TM = 832
SUB = 768


def normalize(matrix):
    centred = matrix - jnp.mean(matrix, axis=-1, keepdims=True)
    inverse = lax.rsqrt(jnp.mean(centred * centred, axis=-1, keepdims=True) + epsilon)
    return (centred * inverse, inverse)


def normalize_back(grad_scaled, normed, inverse):
    mean_grad = jnp.mean(grad_scaled, axis=-1, keepdims=True)
    mean_proj = jnp.mean(grad_scaled * normed, axis=-1, keepdims=True)
    return inverse * (grad_scaled - mean_grad - normed * mean_proj)


def dot(a, b):
    return lax.dot_general(a, b, (((1,), (0,)), ((), ())), preferred_element_type=f32)


def dot_nt(a, b):
    return lax.dot_general(a, b, (((1,), (1,)), ((), ())), preferred_element_type=f32)


def dot_tn(a, b):
    return lax.dot_general(a, b, (((0,), (0,)), ((), ())), preferred_element_type=f32)


def rows_of(ref):
    block = ref[...].astype(f32)
    row = lax.broadcasted_iota(jnp.int32, block.shape, 1)
    return jnp.where(row < L, block, 0.0).reshape(block.shape[0] * RP, D)


def input_projection(x_ref, w_ref, a1_ref, qkv_ref, vec_ref):
    @pl.when(pl.program_id(0) == 0)
    def _():
        vec_ref[...] = w_ref[:, 3 * D :].astype(f32).T[: vec_ref.shape[0]]

    vec = vec_ref[...]
    normed, _ = normalize(rows_of(x_ref))
    a = (normed * vec[GAIN1 : GAIN1 + 1] + vec[SHIFT1 : SHIFT1 + 1]).astype(bf16)
    a1_ref[...] = a
    for h in range(2):
        at = h * HALF
        p = dot(a, w_ref[:, at : at + HALF])
        qb = vec[QB : QB + 1, h * HB : (h + 1) * HB]
        vb = vec[VB : VB + 1, h * HB : (h + 1) * HB]
        qkv_ref[:, at : at + HB] = ((p[:, :HB] + qb) * HD**-0.5).astype(bf16)
        qkv_ref[:, at + HB : at + 2 * HB] = p[:, HB : 2 * HB].astype(bf16)
        qkv_ref[:, at + 2 * HB : at + HALF] = (p[:, 2 * HB :] + vb).astype(bf16)


PAIRS = HB // 128


def place(step):
    t = step // PAIRS
    p = step % PAIRS
    r = pl.ds(pl.multiple_of(t * RP, 16), RP)
    at = lambda k: pl.ds(pl.multiple_of(k * HB + p * 128, 128), 128)
    return t, p, r, at


def forward_attention(qkv_ref, o_ref, lse_ref):
    lane = lax.broadcasted_iota(jnp.int32, (RP, 128), 1)
    key_row = lax.broadcasted_iota(jnp.int32, (RP - EDGE, RP), 0)

    def pair(h, step, carry):
        t, p, r, at = place(step)
        into = pl.ds(pl.multiple_of(h * HB + p * 128, 128), 128)
        at = lambda k: pl.ds(pl.multiple_of(h * HALF + k * HB + p * 128, 128), 128)
        q2 = qkv_ref[r, at(0)]
        k2 = qkv_ref[r, at(1)]
        v2 = qkv_ref[r, at(2)]
        v2t = v2.T
        zero = jnp.zeros_like(k2)
        both = dot_nt(jnp.concatenate([jnp.where(lane < HD, k2, zero), jnp.where(lane < HD, zero, k2)]), q2)
        parts = []
        for hh in range(2):
            s = both[hh * RP : (hh + 1) * RP]
            s = jnp.concatenate([s[:EDGE], jnp.where(key_row < L - EDGE, s[EDGE:], -1e30)], axis=0)
            top = jnp.max(s, axis=0, keepdims=True)
            e = jnp.exp(s - top)
            total = jnp.sum(e, axis=0, keepdims=True)
            w = (e * (1.0 / total)).astype(bf16)
            lse_ref[t, pl.ds(h * (H // 2) + 2 * p + hh, 1), :] = top + jnp.log(total)
            parts.append(dot(v2t[hh * HD : (hh + 1) * HD], w))
        total_t = jnp.concatenate(parts)
        o_ref[r, into] = total_t.T.astype(bf16)
        return carry

    for h in range(2):
        lax.fori_loop(0, lse_ref.shape[0] * PAIRS, functools.partial(pair, h), 0, unroll=UNROLL_F)


def live_rows(count_ref, images):
    shape = (images, RP, D)
    slot = lax.broadcasted_iota(jnp.int32, shape, 0) + pl.program_id(0) * images
    return (slot < count_ref[0]).reshape(images * RP, D)


def output_projection(count_ref, x_ref, c_ref, o_ref, vec_ref, wo_ref, r_ref, a2_ref, cb_ref):
    vec = vec_ref[...]
    live = live_rows(count_ref, x_ref.shape[0])
    cb_ref[...] = jnp.where(live, rows_of(c_ref), 0.0).astype(bf16)
    r = rows_of(x_ref) + vec[OB : OB + 1] + dot(o_ref[...], wo_ref[...])
    r_ref[...] = r
    n2, _ = normalize(r)
    a2_ref[...] = (n2 * vec[GAIN2 : GAIN2 + 1] + vec[SHIFT2 : SHIFT2 + 1]).astype(bf16)


def gelu_parts(z):
    return 0.5 + 0.5 * lax.erf(z * half_root), jnp.exp(z * z * -0.5)


def tiles(rows, body):
    def tile(i, carry):
        body(pl.ds(pl.multiple_of(i * TM, 16), TM))
        return carry

    lax.fori_loop(0, rows // TM, tile, 0)


def hidden(a2_ref, wu_ref, ub_ref, u_ref, slope_ref):
    def body(r):
        a2 = a2_ref[r, :]
        for k in range(D // SUB):
            c = slice(k * SUB, (k + 1) * SUB)
            z = dot(a2, wu_ref[:, c]) + ub_ref[:, c]
            phi, e = gelu_parts(z)
            u_ref[r, c] = (z * phi).astype(bf16)
            slope_ref[r, c] = (phi + z * e * inv_root_tau).astype(bf16)

    tiles(a2_ref.shape[0], body)


def hidden_back(own, cb_ref, packed_ref, u_ref, slope_ref, dz_ref, wd_ref, gwd_ref, gub_ref, cbt):
    if packed_ref.shape == wd_ref.shape:
        wd_ref[...] = packed_ref[...]
    else:
        packed = packed_ref[...].astype(f32)
        parts = [
            packed[d : d + own, k : k + D]
            for d in range(0, packed.shape[0], own) for k in range(0, packed.shape[1], D)
        ]
        wd_ref[...] = jnp.concatenate(parts).astype(bf16)

    @pl.when(pl.program_id(0) == 0)
    def _():
        cbt[...] = cb_ref[...].T

    gub_ref[...] = jnp.zeros_like(gub_ref)

    def body(r):
        dz = (dot_nt(cb_ref[r, :], wd_ref[...]) * slope_ref[r, :].astype(f32)).astype(bf16)
        dz_ref[r, :] = dz
        gub_ref[0] += jnp.sum(dz.astype(f32), axis=0, keepdims=True)

    tiles(cb_ref.shape[0], body)
    gwd_ref[...] = dot(cbt[...], u_ref[...]).T.astype(bf16)


def up_gradient(a2_ref, dz_ref, gwu_ref, a2t):
    @pl.when(pl.program_id(0) == 0)
    def _():
        a2t[...] = a2_ref[...].T

    gwu_ref[...] = dot(a2t[...], dz_ref[...]).astype(bf16)


def middle_back(
    count_ref, r_ref, u_ref, dz_ref, cb_ref, o_ref, vec_ref, wo_ref, wu_ref, wd_ref,
    out_ref, dr_ref, do_ref, gwo_ref, gvec_ref, acc,
):
    step = pl.program_id(0)

    @pl.when(step == 0)
    def _():
        acc[...] = jnp.zeros_like(acc)
        gvec_ref[...] = jnp.zeros_like(gvec_ref)

    vec = vec_ref[...]
    images = out_ref.shape[0]
    live = live_rows(count_ref, images)
    r = r_ref[...]
    out = jnp.where(live, r + dot(u_ref[...], wd_ref[...]) + vec[DB : DB + 1], 0.0)
    out_ref[...] = out.reshape(images, RP, D).astype(bf16)
    n2, i2 = normalize(r)
    da2 = dot_nt(dz_ref[...], wu_ref[...])
    c = cb_ref[...].astype(f32)
    dr = c + normalize_back(da2 * vec[GAIN2 : GAIN2 + 1], n2, i2)
    dr_ref[...] = dr
    drb = dr.astype(bf16)
    for k, m in enumerate((da2 * n2, da2, drb.astype(f32), c)):
        gvec_ref[k : k + 1] += jnp.sum(m, axis=0, keepdims=True)
    acc[...] += dot_tn(o_ref[...], drb)
    do_ref[...] = dot_nt(drb, wo_ref[...]).astype(bf16)

    @pl.when(step == pl.num_programs(0) - 1)
    def _():
        gwo_ref[...] = acc[...].astype(bf16)


def backward_attention(h, qkv_ref, lse_ref, do_ref, a1_ref, *refs):
    dp_ref, gw_ref, gvec_ref, acc = refs[-4:]
    step = pl.program_id(0)
    images = lse_ref.shape[0]

    @pl.when(step == 0)
    def _():
        acc[...] = jnp.zeros_like(acc)
        gvec_ref[...] = jnp.zeros_like(gvec_ref)

    lane = lax.broadcasted_iota(jnp.int32, (RP, 128), 1)
    key_row = lax.broadcasted_iota(jnp.int32, (RP - EDGE, RP), 0)

    def pair(step, carry):
        t, p, r, at = place(step)
        q2 = qkv_ref[r, at(0)]
        k2 = qkv_ref[r, at(1)]
        v2 = qkv_ref[r, at(2)]
        do2 = do_ref[r, at(0)]
        zero = jnp.zeros_like(q2)
        halves = lambda m: jnp.concatenate([jnp.where(lane < HD, m, zero), jnp.where(lane < HD, zero, m)])
        s_both = dot_nt(halves(k2), q2)
        dw_both = dot_nt(halves(v2), do2)
        k2t = k2.T
        ws, dss, dqs = [], [], []
        for hh in range(2):
            s = s_both[hh * RP : (hh + 1) * RP] - lse_ref[t, pl.ds(h * (H // 2) + 2 * p + hh, 1), :]
            dw = dw_both[hh * RP : (hh + 1) * RP]
            s = jnp.concatenate([s[:EDGE], jnp.where(key_row < L - EDGE, s[EDGE:], -1e30)], axis=0)
            w = jnp.exp(s)
            inner = jnp.sum(dw * w, axis=0, keepdims=True)
            ds = (w * (dw - inner)).astype(bf16)
            ws.append(w.astype(bf16))
            dss.append(ds)
            dqs.append(dot(k2t[hh * HD : (hh + 1) * HD], ds))
        dv_both = dot(jnp.concatenate(ws), do2)
        dk_both = dot(jnp.concatenate(dss), q2)
        dv = jnp.where(lane < HD, dv_both[:RP], dv_both[RP:])
        dk = jnp.where(lane < HD, dk_both[:RP], dk_both[RP:])
        dqt = jnp.concatenate(dqs)
        dp_ref[r, at(0)] = (dqt.T * HD**-0.5).astype(bf16)
        dp_ref[r, at(1)] = dk.astype(bf16)
        dp_ref[r, at(2)] = dv.astype(bf16)
        return carry

    lax.fori_loop(0, images * PAIRS, pair, 0, unroll=UNROLL_B)
    acc[...] += dot_tn(a1_ref[...], dp_ref[...])
    gvec_ref[0:1] += jnp.sum(dp_ref[:, :HB].astype(f32), axis=0, keepdims=True)
    gvec_ref[1:2] += jnp.sum(dp_ref[:, 2 * HB :].astype(f32), axis=0, keepdims=True)

    @pl.when(step == pl.num_programs(0) - 1)
    def _():
        gw_ref[:, :HALF] = acc[...].astype(bf16)
        if gw_ref.shape[1] > HALF:
            gw_ref[:, HALF:] = refs[0][...]


def backward_input(
    x_ref, dpa_ref, dpb_ref, dr_ref, vec_ref, w_ref, mid_ref, ga_ref, gb_ref, gub_ref,
    gi_ref, gvec_ref, acc,
):
    step = pl.program_id(0)

    @pl.when(step == 0)
    def _():
        acc[...] = jnp.zeros_like(acc)
        for k, name in enumerate((GAIN2, SHIFT2, OB, DB)):
            acc[name : name + 1] = mid_ref[k : k + 1]
        for k, name in enumerate((QB, VB)):
            acc[name : name + 1, :HB] = ga_ref[k : k + 1]
            acc[name : name + 1, HB:] = gb_ref[k : k + 1]
        acc[UB : UB + gub_ref.shape[0]] = gub_ref[...]

    gain = vec_ref[...][GAIN1 : GAIN1 + 1]
    n1, i1 = normalize(rows_of(x_ref))
    da1 = dot_nt(dpa_ref[...], w_ref[:, :HALF]) + dot_nt(dpb_ref[...], w_ref[:, HALF : 3 * D])
    acc[GAIN1 : GAIN1 + 1] += jnp.sum(da1 * n1, axis=0, keepdims=True)
    acc[SHIFT1 : SHIFT1 + 1] += jnp.sum(da1, axis=0, keepdims=True)
    gi = dr_ref[...] + normalize_back(da1 * gain, n1, i1)
    gi_ref[...] = gi.reshape(x_ref.shape[0], RP, D)

    @pl.when(step == pl.num_programs(0) - 1)
    def _():
        gvec_ref[...] = acc[...].T


def image_spec():
    return pl.BlockSpec((T, RP, D), lambda i: (i, 0, 0))


def row_spec(width, column=0):
    return pl.BlockSpec((T * RP, width), lambda i: (i, column))


def lse_spec():
    return pl.BlockSpec((T, H, RP), lambda i: (i, 0, 0))


def whole(shape, column=0):
    at = (0,) * (len(shape) - 1) + (column,)
    return pl.BlockSpec(shape, lambda i: at, pipeline_mode=pl.Buffered(1))


def launch(body, steps, ins, outs, scratch, deps, flops, moved, ex, name, mib):
    n_in, n_dep, n_out = len(ins), len(deps), len(outs)

    def kernel(*refs):
        token = refs[n_in + n_dep + n_out]
        token[...] = jnp.zeros_like(token)
        first_out = n_in + n_dep
        body(*refs[:n_in], *refs[first_out : first_out + n_out], *refs[first_out + n_out + 1 :])

    results = pl.pallas_call(
        kernel,
        grid=(steps,),
        in_specs=[spec for _, spec in ins] + [pl.BlockSpec(memory_space=pl.ANY)] * n_dep,
        out_specs=[spec for _, _, spec in outs] + [whole((1, 1))],
        out_shape=[jax.ShapeDtypeStruct(shape, kind) for shape, kind, _ in outs]
        + [jax.ShapeDtypeStruct((1, 1), f32)],
        scratch_shapes=scratch,
        compiler_params=pltpu.CompilerParams(
            dimension_semantics=("arbitrary",), vmem_limit_bytes=mib * MIB
        ),
        cost_estimate=pl.CostEstimate(
            flops=int(flops), bytes_accessed=int(moved), transcendentals=int(ex)
        ),
        name=name,
    )(*[a for a, _ in ins], *deps)
    return results[:-1], results[-1].reshape(())


def joined(token, arrays, passed):
    anywhere = pl.BlockSpec(memory_space=pl.ANY)
    one = pl.BlockSpec((1, 1), lambda: (0, 0))
    count = len(passed)

    def kernel(*refs):
        refs[len(refs) - count - 1][...] = refs[0][...]

    token, *passed = pl.pallas_call(
        kernel,
        in_specs=[one] + [anywhere] * (count + len(arrays)),
        out_specs=[one] + [anywhere] * count,
        out_shape=[jax.ShapeDtypeStruct((1, 1), f32)]
        + [jax.ShapeDtypeStruct(p.shape, p.dtype) for p in passed],
        input_output_aliases={k + 1: k + 1 for k in range(count)},
        name="joined",
    )(token.reshape(1, 1), *passed, *arrays)
    return token.reshape(()), passed


class Links:
    def __init__(self, n, me):
        self.n = n
        self.me = me
        self.plane = max(1, min(4, n // 2))
        self.depth = n // (2 * self.plane)
        self.core = me % 2
        self.chip = me // 2 % self.plane
        self.level = me // (2 * self.plane)

    def send(self, a, bits):
        return lax.ppermute(a, "fsdp", [(i, i ^ bits) for i in range(self.n)])

    def across_core(self, a):
        return self.send(a, 1)

    def across_plane(self, a, k):
        return self.send(a, 2 * k)

    def across_depth(self, a, k):
        return self.send(a, 2 * self.plane * k)

    def relative(self, core, k, z):
        return core + 2 * k + 2 * self.plane * z


def copy_blocks(pairs, buffer, in_sems, out_sems):
    arriving = []
    for i, (source, _) in enumerate(pairs):
        arriving.append(pltpu.make_async_copy(source, buffer.at[i], in_sems.at[i]))
        arriving[i].start()
    leaving = []
    for i, (_, target) in enumerate(pairs):
        arriving[i].wait()
        leaving.append(pltpu.make_async_copy(buffer.at[i], target, out_sems.at[i]))
        leaving[i].start()
    for c in leaving:
        c.wait()


def blocks_kernel(body, me, ins, outs, n, block, name):
    anywhere = pl.BlockSpec(memory_space=pl.ANY)
    return pl.pallas_call(
        body,
        in_specs=[pl.BlockSpec(memory_space=pltpu.SMEM)] + [anywhere] * len(ins),
        out_specs=[anywhere] * len(outs),
        out_shape=outs,
        scratch_shapes=[
            pltpu.VMEM((n,) + block, bf16), pltpu.SemaphoreType.DMA((n,)), pltpu.SemaphoreType.DMA((n,))
        ],
        compiler_params=pltpu.CompilerParams(vmem_limit_bytes=40 * MIB),
        cost_estimate=pl.CostEstimate(flops=0, bytes_accessed=8_000_000, transcendentals=0),
        name=name,
    )(me.reshape(1), *ins)


def gather(links, shard, deps):
    n, plane, depth = links.n, links.plane, links.depth
    a = jnp.stack([shard] + [links.across_depth(shard, z) for z in range(1, depth)])
    _, (a,) = joined(jnp.zeros((), f32), deps, [a])
    parts = [a] + [links.across_plane(a, k) for k in range(1, plane)]
    parts = parts + [links.across_core(a) for a in parts]

    def assemble(me_ref, *refs):
        out = refs[2 * plane]
        me = me_ref[0]
        copy_blocks(
            [
                (refs[core * plane + k].at[z], out.at[me ^ links.relative(core, k, z)])
                for core in range(2) for k in range(plane) for z in range(depth)
            ],
            *refs[2 * plane + 1 :],
        )

    out = jax.ShapeDtypeStruct((n,) + shard.shape, shard.dtype)
    whole_rows = blocks_kernel(
        assemble, links.me, parts, [out], n, shard.shape, "assemble"
    )[0]
    return whole_rows.reshape(-1, shard.shape[1])


def pick(a, index, axis):
    return lax.dynamic_index_in_dim(a, index, axis, keepdims=False)


class Scatter:
    def __init__(self, links, a):
        n, plane, depth = links.n, links.plane, links.depth
        self.links = links
        self.blocks = a.reshape(depth, plane, 2, a.shape[0] // n, a.shape[1])
        self.sent = pick(self.blocks, 1 - links.core, 2)
        self.ready = []

    def cores(self):
        self.got = self.links.across_core(self.sent)

    def cores_done(self, token, beside=None):
        links = self.links
        own = pick(self.blocks, links.core, 2)

        def to_chip(k):
            at = links.chip ^ k
            part = pick(own, at, 1).astype(f32) + pick(self.got, at, 1).astype(f32) + token
            if beside is not None:
                part = jnp.concatenate([part, pick(beside, at, 1)], axis=-1)
            return part.astype(bf16)

        self.ready = [to_chip(k) for k in range(links.plane)]

    def planes(self):
        self.got = self.ready[:1] + [
            self.links.across_plane(a, k) for k, a in enumerate(self.ready) if k
        ]

    def planes_done(self, token):
        links = self.links

        def to_level(j):
            at = links.level ^ j
            return (sum(pick(g, at, 0).astype(f32) for g in self.got) + token).astype(bf16)

        self.ready = [to_level(j) for j in range(links.depth)]

    def depths(self):
        self.got = self.ready[:1] + [
            self.links.across_depth(a, j) for j, a in enumerate(self.ready) if j
        ]

    def depths_done(self, token):
        self.result = sum(g.astype(f32) for g in self.got) + token


def pack(own, qkv_ref, columns_ref, out_ref, up_ref, down_ref, first_ref, second_ref):
    for h in range(2):
        for k in range(3):
            at = (3 * h + k) * HB
            first_ref[:, at : at + HB] = qkv_ref[:, k * D + h * HB : k * D + (h + 1) * HB]
    first_ref[:, 3 * D :] = columns_ref[...]
    down = down_ref[...].astype(f32)
    ff = up_ref.shape[1]
    for k in range(down.shape[0] // own):
        second_ref[:, k * D : (k + 1) * D] = down[k * own : (k + 1) * own].astype(bf16)
    second_ref[:, ff : 2 * ff] = up_ref[...]
    second_ref[:, 2 * ff :] = out_ref[...]


def on_device(
    n,
    images,
    counts,
    norm1_gain,
    norm1_bias,
    w_qkv,
    q_bias,
    v_bias,
    w_out,
    out_bias,
    norm2_gain,
    norm2_bias,
    w_up,
    up_bias,
    w_down,
    down_bias,
    cotangent,
):
    links = Links(n, lax.axis_index("fsdp"))
    slots = images.shape[0]
    total = slots * RP
    steps = slots // T
    ff = n * up_bias.shape[0]
    chunks = ff // D
    own = norm1_gain.shape[0]
    own_up = up_bias.shape[0]
    up_rows = own_up // own

    vectors = [norm1_gain, norm1_bias, q_bias, v_bias, out_bias, norm2_gain, norm2_bias, down_bias]
    vectors += [up_bias[k * own : (k + 1) * own] for k in range(up_rows)]
    shape = (len(vectors), own)
    name = lax.broadcasted_iota(jnp.int32, shape, 0)
    columns = jnp.zeros(shape, bf16)
    for k, v in enumerate(vectors):
        columns = jnp.where(name == k, lax.broadcast_in_dim(v, shape, (1,)), columns)
    columns = columns.T
    columns = jnp.pad(columns, ((0, 0), (0, WIDE - 3 * D - columns.shape[1])))
    first, second = pl.pallas_call(
        functools.partial(pack, own),
        out_shape=[jax.ShapeDtypeStruct((own, WIDE), bf16), jax.ShapeDtypeStruct((own, 2 * ff + D), bf16)],
        name="pack",
    )(w_qkv, columns, w_out, w_up, w_down)
    w = gather(links, first, [images, cotangent])
    rest = lax.all_gather(second, "fsdp", axis=0, tiled=True)

    (a1, qkv, vec), _ = launch(
        input_projection, steps,
        [(images, image_spec()), (w, whole((D, WIDE)))],
        [((total, D), bf16, row_spec(D)), ((total, 3 * D), bf16, row_spec(3 * D)),
         ((16, D), f32, whole((16, D)))],
        [], [], total * D * 3 * D * 2, 20e6, 0, "input_projection", 60,
    )
    (o, lse), _ = launch(
        forward_attention, steps,
        [(qkv, row_spec(3 * D))],
        [((total, D), bf16, row_spec(D)), ((slots, H, RP), f32, lse_spec())],
        [], [], slots * H * RP * RP * 256 * 4, 11e6, slots * H * RP * RP, "forward_attention", 60,
    )
    counts_spec = pl.BlockSpec(memory_space=pltpu.SMEM)
    (r, a2, cb), _ = launch(
        output_projection, steps,
        [(counts, counts_spec), (images, image_spec()), (cotangent, image_spec()),
         (o, row_spec(D)), (vec, whole((16, D))), (rest, whole((D, D), 2 * chunks))],
        [((total, D), f32, row_spec(D)), ((total, D), bf16, row_spec(D)),
         ((total, D), bf16, row_spec(D))],
        [], [], total * D * D * 2, 20e6, 0, "output_projection", 60,
    )
    up_shift = vec[UB : UB + up_rows].reshape(up_rows, n, own).transpose(1, 0, 2).reshape(1, ff)
    rows = whole((total, D))
    chunk = pl.BlockSpec((total, D), lambda j: (0, j))
    (u, slope), _ = launch(
        hidden, chunks,
        [(a2, rows), (rest, pl.BlockSpec((D, D), lambda j: (0, j + chunks))),
         (up_shift, pl.BlockSpec((1, D), lambda j: (0, j)))],
        [((total, ff), bf16, chunk), ((total, ff), bf16, chunk)],
        [], [], total * D * ff * 2, 28e6, total * ff, "hidden", 60,
    )
    packed_wd = (rest, pl.BlockSpec((D // up_rows, ff), lambda j: (j, 0)))
    if own % 8:
        wd = rest[:, :ff].reshape(n, own, up_rows, D).transpose(0, 2, 1, 3).reshape(ff, D)
        packed_wd = (wd, pl.BlockSpec((D, D), lambda j: (j, 0)))
    (dz, wd, gwd, gub), _ = launch(
        functools.partial(hidden_back, own), chunks,
        [(cb, rows), packed_wd, (u, chunk), (slope, chunk)],
        [((total, ff), bf16, chunk), ((ff, D), bf16, pl.BlockSpec((D, D), lambda j: (j, 0))),
         ((ff, D), bf16, pl.BlockSpec((D, D), lambda j: (j, 0))),
         ((chunks, 1, D), f32, pl.BlockSpec((1, 1, D), lambda j: (j, 0, 0)))],
        [pltpu.VMEM((D, total), bf16)], [], total * D * ff * 4, 42e6, 0, "hidden_back", 60,
    )
    sd = Scatter(links, gwd)
    (gwu,), token = launch(
        up_gradient, chunks,
        [(a2, rows), (dz, chunk)],
        [((D, ff), bf16, pl.BlockSpec((D, D), lambda j: (0, j)))],
        [pltpu.VMEM((D, total), bf16)], sd.ready, total * D * ff * 2, 18e6, 0, "up_gradient", 60,
    )
    sd.cores()
    sd.cores_done(token)
    su = Scatter(links, gwu)

    (out, dr, do, gwo, gvec_mid), token = launch(
        middle_back, steps,
        [(counts, counts_spec), (r, row_spec(D)), (u, row_spec(ff)), (dz, row_spec(ff)),
         (cb, row_spec(D)), (o, row_spec(D)), (vec, whole((16, D))), (rest, whole((D, D), 2 * chunks)),
         (rest, whole((D, ff), 1)), (wd, whole((ff, D)))],
        [(images.shape, bf16, image_spec()), ((total, D), f32, row_spec(D)),
         ((total, D), bf16, row_spec(D)), ((D, D), bf16, whole((D, D))), ((8, D), f32, whole((8, D)))],
        [pltpu.VMEM((D, D), f32)], sd.ready + su.ready, total * D * (ff + D) * 4, 50e6, 0, "middle_back", 60,
    )
    sd.planes()
    su.cores()
    sd.planes_done(token)
    su.cores_done(token)

    def attention_back(h, carried, deps):
        width = HALF + D * len(carried)
        return launch(
            functools.partial(backward_attention, h), steps,
            [(qkv, row_spec(HALF, h)), (lse, lse_spec()), (do, row_spec(HB, h)), (a1, row_spec(D))]
            + [(a, whole((D, D))) for a in carried],
            [((total, HALF), bf16, row_spec(HALF)), ((D, width), bf16, whole((D, width))),
             ((8, HB), f32, whole((8, HB)))],
            [pltpu.VMEM((D, HALF), f32)], deps,
            total * D * HALF * 2 + slots * H * RP * RP * 256 * 5, 14e6, slots * H * RP * RP // 2,
            "backward_attention", 60,
        )

    (dpa, gwa, gvec_a), token = attention_back(0, [gwo], sd.ready + su.ready)
    su.planes()
    sd.depths()
    su.planes_done(token)
    sd.depths_done(token)
    sa = Scatter(links, gwa)
    (dpb, gwb, gvec_b), token = attention_back(1, [], su.ready + sa.ready)
    su.depths()
    sa.cores()
    su.depths_done(token)
    sa.cores_done(token)
    sb = Scatter(links, gwb)
    gub = gub.reshape(n, up_rows, own).transpose(1, 0, 2).reshape(up_rows, D)
    (gi, gvec), token = launch(
        backward_input, steps,
        [(images, image_spec()), (dpa, row_spec(HALF)), (dpb, row_spec(HALF)), (dr, row_spec(D)),
         (vec, whole((16, D))), (w, whole((D, WIDE))), (gvec_mid, whole((8, D))),
         (gvec_a, whole((8, HB))), (gvec_b, whole((8, HB))), (gub, whole((up_rows, D)))],
        [(images.shape, f32, image_spec()), ((D, 128), f32, whole((D, 128)))],
        [pltpu.VMEM((128, D), f32)], sa.ready + sb.ready, total * D * 3 * D * 2, 25e6, 0, "backward_input", 60,
    )
    sa.planes()
    sb.cores()
    token, (out, gi, gvec) = joined(token, sa.got[1:], [out, gi, gvec])
    gvec = gvec.reshape(links.depth, links.plane, 2, own, 128)
    gvec = pick(gvec, links.core, 2) + links.across_core(pick(gvec, 1 - links.core, 2))
    sb.cores_done(token, gvec)
    sb.planes()
    sa.planes_done(token)
    zero = jnp.zeros((), f32)
    sb.planes_done(zero)
    sb.ready = [jnp.concatenate([x, y], axis=-1) for x, y in zip(sa.ready, sb.ready)]
    sb.depths()
    sb.depths_done(zero)
    fa, fb = sb.result[:, : HALF + D], sb.result[:, HALF + D :]
    shard_up, shard_down = su.result, sd.result
    shard_qkv = jnp.concatenate(
        [f[:, k * HB : (k + 1) * HB] for k in range(3) for f in (fa, fb)], axis=1
    )
    shard_out = fa[:, HALF:]
    small = fb[:, HALF : HALF + UB + up_rows].T
    shard_up_shift = small[UB:].reshape(own_up)
    return (
        out,
        gi,
        small[GAIN1],
        small[SHIFT1],
        shard_qkv,
        small[QB],
        small[VB],
        shard_out,
        small[OB],
        small[GAIN2],
        small[SHIFT2],
        shard_up,
        shard_up_shift,
        shard_down,
        small[DB],
    )


def solution(mesh):
    rows = P("fsdp", None)
    cube = P("fsdp", None, None)
    one = P("fsdp")
    return jax.shard_map(
        functools.partial(on_device, mesh.shape["fsdp"]),
        mesh=mesh,
        in_specs=(cube, one, one, one, rows, one, one, rows, one, one, one, rows, one, rows, one, cube),
        out_specs=(cube, cube, one, one, rows, one, one, rows, one, one, one, rows, one, rows, one),
        check_vma=False,
    )
```

```python
import functools

import jax
import jax.numpy as jnp
from jax import lax
from jax.experimental import pallas as pl
from jax.experimental.pallas import tpu as pltpu
from jax.sharding import PartitionSpec as P

D = 768
H = 12
HD = 64
L = 197
RP = 208
HALF = 3 * D // 2
WIDE = 3 * D + 128
HB = D // 2
EDGE = L // 8 * 8
T = 2
GAIN1, SHIFT1, QB, VB, OB, GAIN2, SHIFT2, DB, UB = range(9)

epsilon = 1e-06
half_root = 0.7071067811865476
inv_root_tau = 0.3989422804014327
f32 = jnp.float32
bf16 = jnp.bfloat16
MIB = 1 << 20


UNROLL_F = 6
UNROLL_B = 6
TM = 8 * RP
SUB = 768


def normalize(matrix):
    centred = matrix - jnp.mean(matrix, axis=-1, keepdims=True)
    inverse = lax.rsqrt(jnp.mean(centred * centred, axis=-1, keepdims=True) + epsilon)
    return (centred * inverse, inverse)


def normalize_back(grad_scaled, normed, inverse):
    mean_grad = jnp.mean(grad_scaled, axis=-1, keepdims=True)
    mean_proj = jnp.mean(grad_scaled * normed, axis=-1, keepdims=True)
    return inverse * (grad_scaled - mean_grad - normed * mean_proj)


def dot(a, b):
    return lax.dot_general(a, b, (((1,), (0,)), ((), ())), preferred_element_type=f32)


def dot_nt(a, b):
    return lax.dot_general(a, b, (((1,), (1,)), ((), ())), preferred_element_type=f32)


def dot_tn(a, b):
    return lax.dot_general(a, b, (((0,), (0,)), ((), ())), preferred_element_type=f32)


def rows_of(ref):
    block = ref[...].astype(f32)
    row = lax.broadcasted_iota(jnp.int32, block.shape, 1)
    return jnp.where(row < L, block, 0.0).reshape(block.shape[0] * RP, D)


def input_projection(x_ref, w_ref, a1_ref, qkv_ref, vec_ref):
    @pl.when(pl.program_id(0) == 0)
    def _():
        vec_ref[...] = w_ref[:, 3 * D :].astype(f32).T[: vec_ref.shape[0]]

    vec = vec_ref[...]
    normed, _ = normalize(rows_of(x_ref))
    a = (normed * vec[GAIN1 : GAIN1 + 1] + vec[SHIFT1 : SHIFT1 + 1]).astype(bf16)
    a1_ref[...] = a
    for h in range(2):
        at = h * HALF
        p = dot(a, w_ref[:, at : at + HALF])
        qb = vec[QB : QB + 1, h * HB : (h + 1) * HB]
        vb = vec[VB : VB + 1, h * HB : (h + 1) * HB]
        qkv_ref[:, at : at + HB] = ((p[:, :HB] + qb) * HD**-0.5).astype(bf16)
        qkv_ref[:, at + HB : at + 2 * HB] = p[:, HB : 2 * HB].astype(bf16)
        qkv_ref[:, at + 2 * HB : at + HALF] = (p[:, 2 * HB :] + vb).astype(bf16)


PAIRS = HB // 128


def place(step):
    t = step // PAIRS
    p = step % PAIRS
    r = pl.ds(pl.multiple_of(t * RP, 16), RP)
    at = lambda k: pl.ds(pl.multiple_of(k * HB + p * 128, 128), 128)
    return t, p, r, at


def forward_attention(qkv_ref, o_ref, lse_ref):
    lane = lax.broadcasted_iota(jnp.int32, (RP, 128), 1)
    key_row = lax.broadcasted_iota(jnp.int32, (RP - EDGE, RP), 0)

    def pair(h, step, carry):
        t, p, r, at = place(step)
        into = pl.ds(pl.multiple_of(h * HB + p * 128, 128), 128)
        at = lambda k: pl.ds(pl.multiple_of(h * HALF + k * HB + p * 128, 128), 128)
        q2 = qkv_ref[r, at(0)]
        k2 = qkv_ref[r, at(1)]
        v2 = qkv_ref[r, at(2)]
        v2t = v2.T
        zero = jnp.zeros_like(k2)
        both = dot_nt(jnp.concatenate([jnp.where(lane < HD, k2, zero), jnp.where(lane < HD, zero, k2)]), q2)
        parts = []
        for hh in range(2):
            s = both[hh * RP : (hh + 1) * RP]
            s = jnp.concatenate([s[:EDGE], jnp.where(key_row < L - EDGE, s[EDGE:], -1e30)], axis=0)
            top = jnp.max(s, axis=0, keepdims=True)
            e = jnp.exp(s - top)
            total = jnp.sum(e, axis=0, keepdims=True)
            w = (e * (1.0 / total)).astype(bf16)
            lse_ref[t, pl.ds(h * (H // 2) + 2 * p + hh, 1), :] = top + jnp.log(total)
            parts.append(dot(v2t[hh * HD : (hh + 1) * HD], w))
        total_t = jnp.concatenate(parts)
        o_ref[r, into] = total_t.T.astype(bf16)
        return carry

    for h in range(2):
        lax.fori_loop(0, lse_ref.shape[0] * PAIRS, functools.partial(pair, h), 0, unroll=UNROLL_F)


def live_rows(count_ref, images):
    shape = (images, RP, D)
    slot = lax.broadcasted_iota(jnp.int32, shape, 0) + pl.program_id(0) * images
    return (slot < count_ref[0]).reshape(images * RP, D)


def output_projection(count_ref, x_ref, c_ref, o_ref, vec_ref, wo_ref, r_ref, a2_ref, cb_ref):
    vec = vec_ref[...]
    live = live_rows(count_ref, x_ref.shape[0])
    cb_ref[...] = jnp.where(live, rows_of(c_ref), 0.0).astype(bf16)
    r = rows_of(x_ref) + vec[OB : OB + 1] + dot(o_ref[...], wo_ref[...])
    r_ref[...] = r
    n2, _ = normalize(r)
    a2_ref[...] = (n2 * vec[GAIN2 : GAIN2 + 1] + vec[SHIFT2 : SHIFT2 + 1]).astype(bf16)


def gelu_parts(z):
    return 0.5 + 0.5 * lax.erf(z * half_root), jnp.exp(z * z * -0.5)


def tiles(rows, body):
    def tile(i, carry):
        body(pl.ds(pl.multiple_of(i * TM, 16), TM))
        return carry

    lax.fori_loop(0, rows // TM, tile, 0)


def hidden(a2_ref, wu_ref, ub_ref, u_ref, slope_ref):
    def body(r):
        a2 = a2_ref[r, :]
        for k in range(D // SUB):
            c = slice(k * SUB, (k + 1) * SUB)
            z = dot(a2, wu_ref[:, c]) + ub_ref[:, c]
            phi, e = gelu_parts(z)
            u_ref[r, c] = (z * phi).astype(bf16)
            slope_ref[r, c] = (phi + z * e * inv_root_tau).astype(bf16)

    tiles(a2_ref.shape[0], body)


def hidden_back(own, cb_ref, packed_ref, u_ref, slope_ref, dz_ref, wd_ref, gwd_ref, gub_ref, cbt, total_ref):
    if packed_ref.shape == wd_ref.shape:
        wd_ref[...] = packed_ref[...]
    else:
        packed = packed_ref[...].astype(f32)
        parts = [
            packed[d : d + own, k : k + D]
            for d in range(0, packed.shape[0], own) for k in range(0, packed.shape[1], D)
        ]
        wd_ref[...] = jnp.concatenate(parts).astype(bf16)

    @pl.when(pl.program_id(0) == 0)
    def _():
        cbt[...] = cb_ref[...].T

    total_ref[...] = jnp.zeros_like(total_ref)

    def body(r):
        dz = (dot_nt(cb_ref[r, :], wd_ref[...]) * slope_ref[r, :].astype(f32)).astype(bf16)
        dz_ref[r, :] = dz
        total_ref[...] += jnp.sum(dz.astype(f32), axis=0, keepdims=True)

    tiles(cb_ref.shape[0], body)
    if gub_ref.shape[1] > 1:
        sums = total_ref[...]
        for q in range(gub_ref.shape[1]):
            starts = range(q * own, D, own * gub_ref.shape[1])
            gub_ref[0, q : q + 1, :] = jnp.concatenate([sums[:, k : k + own] for k in starts], axis=1)
    else:
        gub_ref[0] = total_ref[...]
    gwd_ref[...] = dot(cbt[...], u_ref[...]).T.astype(bf16)


def up_gradient(a2_ref, dz_ref, gwu_ref, a2t):
    @pl.when(pl.program_id(0) == 0)
    def _():
        a2t[...] = a2_ref[...].T

    gwu_ref[...] = dot(a2t[...], dz_ref[...]).astype(bf16)


def middle_back(
    count_ref, r_ref, u_ref, dz_ref, cb_ref, o_ref, vec_ref, wo_ref, wu_ref, wd_ref,
    out_ref, dr_ref, do_ref, gwo_ref, gvec_ref, acc,
):
    step = pl.program_id(0)

    @pl.when(step == 0)
    def _():
        acc[...] = jnp.zeros_like(acc)
        gvec_ref[...] = jnp.zeros_like(gvec_ref)

    vec = vec_ref[...]
    images = out_ref.shape[0]
    live = live_rows(count_ref, images)
    r = r_ref[...]
    out = jnp.where(live, r + dot(u_ref[...], wd_ref[...]) + vec[DB : DB + 1], 0.0)
    out_ref[...] = out.reshape(images, RP, D).astype(bf16)
    n2, i2 = normalize(r)
    da2 = dot_nt(dz_ref[...], wu_ref[...])
    c = cb_ref[...].astype(f32)
    dr = c + normalize_back(da2 * vec[GAIN2 : GAIN2 + 1], n2, i2)
    dr_ref[...] = dr
    drb = dr.astype(bf16)
    for k, m in enumerate((da2 * n2, da2, drb.astype(f32), c)):
        gvec_ref[k : k + 1] += jnp.sum(m, axis=0, keepdims=True)
    acc[...] += dot_tn(o_ref[...], drb)
    do_ref[...] = dot_nt(drb, wo_ref[...]).astype(bf16)

    @pl.when(step == pl.num_programs(0) - 1)
    def _():
        gwo_ref[...] = acc[...].astype(bf16)


def backward_attention(h, qkv_ref, lse_ref, do_ref, a1_ref, *refs):
    dp_ref, gw_ref, gvec_ref, acc = refs[-4:]
    step = pl.program_id(0)
    images = lse_ref.shape[0]

    @pl.when(step == 0)
    def _():
        acc[...] = jnp.zeros_like(acc)
        gvec_ref[...] = jnp.zeros_like(gvec_ref)

    lane = lax.broadcasted_iota(jnp.int32, (RP, 128), 1)
    key_row = lax.broadcasted_iota(jnp.int32, (RP - EDGE, RP), 0)

    def pair(step, carry):
        t, p, r, at = place(step)
        q2 = qkv_ref[r, at(0)]
        k2 = qkv_ref[r, at(1)]
        v2 = qkv_ref[r, at(2)]
        do2 = do_ref[r, at(0)]
        zero = jnp.zeros_like(q2)
        halves = lambda m: jnp.concatenate([jnp.where(lane < HD, m, zero), jnp.where(lane < HD, zero, m)])
        s_both = dot_nt(halves(k2), q2)
        dw_both = dot_nt(halves(v2), do2)
        k2t = k2.T
        ws, dss, dqs = [], [], []
        for hh in range(2):
            s = s_both[hh * RP : (hh + 1) * RP] - lse_ref[t, pl.ds(h * (H // 2) + 2 * p + hh, 1), :]
            dw = dw_both[hh * RP : (hh + 1) * RP]
            s = jnp.concatenate([s[:EDGE], jnp.where(key_row < L - EDGE, s[EDGE:], -1e30)], axis=0)
            w = jnp.exp(s)
            inner = jnp.sum(dw * w, axis=0, keepdims=True)
            ds = (w * (dw - inner)).astype(bf16)
            ws.append(w.astype(bf16))
            dss.append(ds)
            dqs.append(dot(k2t[hh * HD : (hh + 1) * HD], ds))
        dv_both = dot(jnp.concatenate(ws), do2)
        dk_both = dot(jnp.concatenate(dss), q2)
        dv = jnp.where(lane < HD, dv_both[:RP], dv_both[RP:])
        dk = jnp.where(lane < HD, dk_both[:RP], dk_both[RP:])
        dqt = jnp.concatenate(dqs)
        dp_ref[r, at(0)] = (dqt.T * HD**-0.5).astype(bf16)
        dp_ref[r, at(1)] = dk.astype(bf16)
        dp_ref[r, at(2)] = dv.astype(bf16)
        return carry

    lax.fori_loop(0, images * PAIRS, pair, 0, unroll=UNROLL_B)
    acc[...] += dot_tn(a1_ref[...], dp_ref[...])
    gvec_ref[0:1] += jnp.sum(dp_ref[:, :HB].astype(f32), axis=0, keepdims=True)
    gvec_ref[1:2] += jnp.sum(dp_ref[:, 2 * HB :].astype(f32), axis=0, keepdims=True)

    @pl.when(step == pl.num_programs(0) - 1)
    def _():
        gw_ref[:, :HALF] = acc[...].astype(bf16)
        if gw_ref.shape[1] > HALF:
            gw_ref[:, HALF:] = refs[0][...]


def backward_input(
    x_ref, dpa_ref, dpb_ref, dr_ref, vec_ref, w_ref, mid_ref, ga_ref, gb_ref, gub_ref,
    gi_ref, gvec_ref, acc,
):
    step = pl.program_id(0)

    @pl.when(step == 0)
    def _():
        acc[...] = jnp.zeros_like(acc)
        for k, name in enumerate((GAIN2, SHIFT2, OB, DB)):
            acc[name : name + 1] = mid_ref[k : k + 1]
        for k, name in enumerate((QB, VB)):
            acc[name : name + 1, :HB] = ga_ref[k : k + 1]
            acc[name : name + 1, HB:] = gb_ref[k : k + 1]
        for j in range(gub_ref.shape[0]):
            wide = gub_ref.shape[2]
            acc[UB : UB + gub_ref.shape[1], j * wide : (j + 1) * wide] = gub_ref[j]

    gain = vec_ref[...][GAIN1 : GAIN1 + 1]
    n1, i1 = normalize(rows_of(x_ref))
    da1 = dot_nt(dpa_ref[...], w_ref[:, :HALF]) + dot_nt(dpb_ref[...], w_ref[:, HALF : 3 * D])
    acc[GAIN1 : GAIN1 + 1] += jnp.sum(da1 * n1, axis=0, keepdims=True)
    acc[SHIFT1 : SHIFT1 + 1] += jnp.sum(da1, axis=0, keepdims=True)
    gi = dr_ref[...] + normalize_back(da1 * gain, n1, i1)
    gi_ref[...] = gi.reshape(x_ref.shape[0], RP, D)

    @pl.when(step == pl.num_programs(0) - 1)
    def _():
        gvec_ref[...] = acc[...].T


def image_spec():
    return pl.BlockSpec((T, RP, D), lambda i: (i, 0, 0))


def row_spec(width, column=0):
    return pl.BlockSpec((T * RP, width), lambda i: (i, column))


def lse_spec():
    return pl.BlockSpec((T, H, RP), lambda i: (i, 0, 0))


def whole(shape, column=0):
    at = (0,) * (len(shape) - 1) + (column,)
    return pl.BlockSpec(shape, lambda i: at, pipeline_mode=pl.Buffered(1))


def launch(body, steps, ins, outs, scratch, deps, flops, moved, ex, name, mib):
    n_in, n_dep, n_out = len(ins), len(deps), len(outs)

    def kernel(*refs):
        token = refs[n_in + n_dep + n_out]
        token[...] = jnp.zeros_like(token)
        first_out = n_in + n_dep
        body(*refs[:n_in], *refs[first_out : first_out + n_out], *refs[first_out + n_out + 1 :])

    results = pl.pallas_call(
        kernel,
        grid=(steps,),
        in_specs=[spec for _, spec in ins] + [pl.BlockSpec(memory_space=pl.ANY)] * n_dep,
        out_specs=[spec for _, _, spec in outs] + [whole((1, 1))],
        out_shape=[jax.ShapeDtypeStruct(shape, kind) for shape, kind, _ in outs]
        + [jax.ShapeDtypeStruct((1, 1), f32)],
        scratch_shapes=scratch,
        compiler_params=pltpu.CompilerParams(
            dimension_semantics=("arbitrary",), vmem_limit_bytes=mib * MIB
        ),
        cost_estimate=pl.CostEstimate(
            flops=int(flops), bytes_accessed=int(moved), transcendentals=int(ex)
        ),
        name=name,
    )(*[a for a, _ in ins], *deps)
    return results[:-1], results[-1].reshape(())


def joined(token, arrays, passed):
    anywhere = pl.BlockSpec(memory_space=pl.ANY)
    one = pl.BlockSpec((1, 1), lambda: (0, 0))
    count = len(passed)

    def kernel(*refs):
        refs[len(refs) - count - 1][...] = refs[0][...]

    token, *passed = pl.pallas_call(
        kernel,
        in_specs=[one] + [anywhere] * (count + len(arrays)),
        out_specs=[one] + [anywhere] * count,
        out_shape=[jax.ShapeDtypeStruct((1, 1), f32)]
        + [jax.ShapeDtypeStruct(p.shape, p.dtype) for p in passed],
        input_output_aliases={k + 1: k + 1 for k in range(count)},
        name="joined",
    )(token.reshape(1, 1), *passed, *arrays)
    return token.reshape(()), passed


class Links:
    def __init__(self, n, me):
        self.n = n
        self.me = me
        self.plane = max(1, min(4, n // 2))
        self.depth = n // (2 * self.plane)
        self.core = me % 2
        self.chip = me // 2 % self.plane
        self.level = me // (2 * self.plane)

    def send(self, a, bits):
        return lax.ppermute(a, "fsdp", [(i, i ^ bits) for i in range(self.n)])

    def across_core(self, a):
        return self.send(a, 1)

    def across_plane(self, a, k):
        return self.send(a, 2 * k)

    def across_depth(self, a, k):
        return self.send(a, 2 * self.plane * k)

    def relative(self, core, k, z):
        return core + 2 * k + 2 * self.plane * z


def copy_blocks(pairs, buffer, in_sems, out_sems):
    arriving = []
    for i, (source, _) in enumerate(pairs):
        arriving.append(pltpu.make_async_copy(source, buffer.at[i], in_sems.at[i]))
        arriving[i].start()
    leaving = []
    for i, (_, target) in enumerate(pairs):
        arriving[i].wait()
        leaving.append(pltpu.make_async_copy(buffer.at[i], target, out_sems.at[i]))
        leaving[i].start()
    for c in leaving:
        c.wait()


def blocks_kernel(body, me, ins, outs, n, block, name):
    anywhere = pl.BlockSpec(memory_space=pl.ANY)
    return pl.pallas_call(
        body,
        in_specs=[pl.BlockSpec(memory_space=pltpu.SMEM)] + [anywhere] * len(ins),
        out_specs=[anywhere] * len(outs),
        out_shape=outs,
        scratch_shapes=[
            pltpu.VMEM((n,) + block, bf16), pltpu.SemaphoreType.DMA((n,)), pltpu.SemaphoreType.DMA((n,))
        ],
        compiler_params=pltpu.CompilerParams(vmem_limit_bytes=40 * MIB),
        cost_estimate=pl.CostEstimate(flops=0, bytes_accessed=8_000_000, transcendentals=0),
        name=name,
    )(me.reshape(1), *ins)


def gather(links, shard, deps):
    n, plane, depth = links.n, links.plane, links.depth
    a = jnp.stack([shard] + [links.across_depth(shard, z) for z in range(1, depth)])
    _, (a,) = joined(jnp.zeros((), f32), deps, [a])
    parts = [a] + [links.across_plane(a, k) for k in range(1, plane)]
    parts = parts + [links.across_core(a) for a in parts]

    def assemble(me_ref, *refs):
        out = refs[2 * plane]
        me = me_ref[0]
        copy_blocks(
            [
                (refs[core * plane + k].at[z], out.at[me ^ links.relative(core, k, z)])
                for core in range(2) for k in range(plane) for z in range(depth)
            ],
            *refs[2 * plane + 1 :],
        )

    out = jax.ShapeDtypeStruct((n,) + shard.shape, shard.dtype)
    whole_rows = blocks_kernel(
        assemble, links.me, parts, [out], n, shard.shape, "assemble"
    )[0]
    return whole_rows.reshape(-1, shard.shape[1])


def pick(a, index, axis):
    return lax.dynamic_index_in_dim(a, index, axis, keepdims=False)


class Scatter:
    def __init__(self, links, a):
        n, plane, depth = links.n, links.plane, links.depth
        self.links = links
        self.blocks = a.reshape(depth, plane, 2, a.shape[0] // n, a.shape[1])
        self.sent = pick(self.blocks, 1 - links.core, 2)
        self.ready = []

    def cores(self):
        self.got = self.links.across_core(self.sent)

    def cores_done(self, token, beside=None):
        links = self.links
        own = pick(self.blocks, links.core, 2)

        def to_chip(k):
            at = links.chip ^ k
            part = pick(own, at, 1).astype(f32) + pick(self.got, at, 1).astype(f32) + token
            if beside is not None:
                part = jnp.concatenate([part, pick(beside, at, 1)], axis=-1)
            return part.astype(bf16)

        self.ready = [to_chip(k) for k in range(links.plane)]

    def planes(self):
        self.got = self.ready[:1] + [
            self.links.across_plane(a, k) for k, a in enumerate(self.ready) if k
        ]

    def planes_done(self, token):
        links = self.links

        def to_level(j):
            at = links.level ^ j
            return (sum(pick(g, at, 0).astype(f32) for g in self.got) + token).astype(bf16)

        self.ready = [to_level(j) for j in range(links.depth)]

    def depths(self):
        self.got = self.ready[:1] + [
            self.links.across_depth(a, j) for j, a in enumerate(self.ready) if j
        ]

    def depths_done(self, token):
        self.result = sum(g.astype(f32) for g in self.got) + token


def pack(own, qkv_ref, columns_ref, out_ref, up_ref, down_ref, first_ref, second_ref):
    for h in range(2):
        for k in range(3):
            at = (3 * h + k) * HB
            first_ref[:, at : at + HB] = qkv_ref[:, k * D + h * HB : k * D + (h + 1) * HB]
    first_ref[:, 3 * D :] = columns_ref[...]
    down = down_ref[...].astype(f32)
    ff = up_ref.shape[1]
    for k in range(down.shape[0] // own):
        second_ref[:, k * D : (k + 1) * D] = down[k * own : (k + 1) * own].astype(bf16)
    second_ref[:, ff : 2 * ff] = up_ref[...]
    second_ref[:, 2 * ff :] = out_ref[...]


def on_device(
    n,
    images,
    counts,
    norm1_gain,
    norm1_bias,
    w_qkv,
    q_bias,
    v_bias,
    w_out,
    out_bias,
    norm2_gain,
    norm2_bias,
    w_up,
    up_bias,
    w_down,
    down_bias,
    cotangent,
):
    links = Links(n, lax.axis_index("fsdp"))
    slots = images.shape[0]
    total = slots * RP
    steps = slots // T
    ff = n * up_bias.shape[0]
    chunks = ff // D
    own = norm1_gain.shape[0]
    own_up = up_bias.shape[0]
    up_rows = own_up // own

    vectors = [norm1_gain, norm1_bias, q_bias, v_bias, out_bias, norm2_gain, norm2_bias, down_bias]
    vectors += [up_bias[k * own : (k + 1) * own] for k in range(up_rows)]
    shape = (len(vectors), own)
    name = lax.broadcasted_iota(jnp.int32, shape, 0)
    columns = jnp.zeros(shape, bf16)
    for k, v in enumerate(vectors):
        columns = jnp.where(name == k, lax.broadcast_in_dim(v, shape, (1,)), columns)
    columns = columns.T
    columns = jnp.pad(columns, ((0, 0), (0, WIDE - 3 * D - columns.shape[1])))
    first, second = pl.pallas_call(
        functools.partial(pack, own),
        out_shape=[jax.ShapeDtypeStruct((own, WIDE), bf16), jax.ShapeDtypeStruct((own, 2 * ff + D), bf16)],
        name="pack",
    )(w_qkv, columns, w_out, w_up, w_down)
    w = gather(links, first, [images, cotangent])
    rest = lax.all_gather(second, "fsdp", axis=0, tiled=True)

    (a1, qkv, vec), _ = launch(
        input_projection, steps,
        [(images, image_spec()), (w, whole((D, WIDE)))],
        [((total, D), bf16, row_spec(D)), ((total, 3 * D), bf16, row_spec(3 * D)),
         ((16, D), f32, whole((16, D)))],
        [], [], total * D * 3 * D * 2, 20e6, 0, "input_projection", 60,
    )
    (o, lse), _ = launch(
        forward_attention, steps,
        [(qkv, row_spec(3 * D))],
        [((total, D), bf16, row_spec(D)), ((slots, H, RP), f32, lse_spec())],
        [], [], slots * H * RP * RP * 256 * 4, 11e6, slots * H * RP * RP, "forward_attention", 60,
    )
    counts_spec = pl.BlockSpec(memory_space=pltpu.SMEM)
    (r, a2, cb), _ = launch(
        output_projection, steps,
        [(counts, counts_spec), (images, image_spec()), (cotangent, image_spec()),
         (o, row_spec(D)), (vec, whole((16, D))), (rest, whole((D, D), 2 * chunks))],
        [((total, D), f32, row_spec(D)), ((total, D), bf16, row_spec(D)),
         ((total, D), bf16, row_spec(D))],
        [], [], total * D * D * 2, 20e6, 0, "output_projection", 60,
    )
    up_shift = vec[UB : UB + up_rows].reshape(up_rows, n, own).transpose(1, 0, 2).reshape(1, ff)
    rows = whole((total, D))
    chunk = pl.BlockSpec((total, D), lambda j: (0, j))
    (u, slope), _ = launch(
        hidden, chunks,
        [(a2, rows), (rest, pl.BlockSpec((D, D), lambda j: (0, j + chunks))),
         (up_shift, pl.BlockSpec((1, D), lambda j: (0, j)))],
        [((total, ff), bf16, chunk), ((total, ff), bf16, chunk)],
        [], [], total * D * ff * 2, 28e6, total * ff, "hidden", 60,
    )
    packed_wd = (rest, pl.BlockSpec((D // up_rows, ff), lambda j: (j, 0)))
    if own % 8:
        wd = rest[:, :ff].reshape(n, own, up_rows, D).transpose(0, 2, 1, 3).reshape(ff, D)
        packed_wd = (wd, pl.BlockSpec((D, D), lambda j: (j, 0)))
    gub_shape = (1, D) if own % 8 else (up_rows, D // up_rows)
    (dz, wd, gwd, gub), _ = launch(
        functools.partial(hidden_back, own), chunks,
        [(cb, rows), packed_wd, (u, chunk), (slope, chunk)],
        [((total, ff), bf16, chunk), ((ff, D), bf16, pl.BlockSpec((D, D), lambda j: (j, 0))),
         ((ff, D), bf16, pl.BlockSpec((D, D), lambda j: (j, 0))),
         ((chunks,) + gub_shape, f32, pl.BlockSpec((1,) + gub_shape, lambda j: (j, 0, 0)))],
        [pltpu.VMEM((D, total), bf16), pltpu.VMEM((1, D), f32)], [], total * D * ff * 4, 42e6, 0, "hidden_back", 60,
    )
    sd = Scatter(links, gwd)
    (gwu,), token = launch(
        up_gradient, chunks,
        [(a2, rows), (dz, chunk)],
        [((D, ff), bf16, pl.BlockSpec((D, D), lambda j: (0, j)))],
        [pltpu.VMEM((D, total), bf16)], sd.ready, total * D * ff * 2, 18e6, 0, "up_gradient", 60,
    )
    sd.cores()
    sd.cores_done(token)
    su = Scatter(links, gwu)

    (out, dr, do, gwo, gvec_mid), token = launch(
        middle_back, steps,
        [(counts, counts_spec), (r, row_spec(D)), (u, row_spec(ff)), (dz, row_spec(ff)),
         (cb, row_spec(D)), (o, row_spec(D)), (vec, whole((16, D))), (rest, whole((D, D), 2 * chunks)),
         (rest, whole((D, ff), 1)), (wd, whole((ff, D)))],
        [(images.shape, bf16, image_spec()), ((total, D), f32, row_spec(D)),
         ((total, D), bf16, row_spec(D)), ((D, D), bf16, whole((D, D))), ((8, D), f32, whole((8, D)))],
        [pltpu.VMEM((D, D), f32)], sd.ready + su.ready, total * D * (ff + D) * 4, 50e6, 0, "middle_back", 60,
    )
    sd.planes()
    su.cores()
    sd.planes_done(token)
    su.cores_done(token)

    def attention_back(h, carried, deps):
        width = HALF + D * len(carried)
        return launch(
            functools.partial(backward_attention, h), steps,
            [(qkv, row_spec(HALF, h)), (lse, lse_spec()), (do, row_spec(HB, h)), (a1, row_spec(D))]
            + [(a, whole((D, D))) for a in carried],
            [((total, HALF), bf16, row_spec(HALF)), ((D, width), bf16, whole((D, width))),
             ((8, HB), f32, whole((8, HB)))],
            [pltpu.VMEM((D, HALF), f32)], deps,
            total * D * HALF * 2 + slots * H * RP * RP * 256 * 5, 14e6, slots * H * RP * RP // 2,
            "backward_attention", 60,
        )

    (dpa, gwa, gvec_a), token = attention_back(0, [gwo], sd.ready + su.ready)
    su.planes()
    sd.depths()
    su.planes_done(token)
    sd.depths_done(token)
    sa = Scatter(links, gwa)
    (dpb, gwb, gvec_b), token = attention_back(1, [], su.ready + sa.ready)
    su.depths()
    sa.cores()
    su.depths_done(token)
    sa.cores_done(token)
    sb = Scatter(links, gwb)
    if own % 8:
        gub = gub.reshape(n, up_rows, own).transpose(1, 0, 2).reshape(up_rows, D)
        gub = gub.reshape(up_rows, chunks, D // chunks).transpose(1, 0, 2)
    (gi, gvec), token = launch(
        backward_input, steps,
        [(images, image_spec()), (dpa, row_spec(HALF)), (dpb, row_spec(HALF)), (dr, row_spec(D)),
         (vec, whole((16, D))), (w, whole((D, WIDE))), (gvec_mid, whole((8, D))),
         (gvec_a, whole((8, HB))), (gvec_b, whole((8, HB))), (gub, whole((chunks, up_rows, D // chunks)))],
        [(images.shape, f32, image_spec()), ((D, 128), f32, whole((D, 128)))],
        [pltpu.VMEM((128, D), f32)], sa.ready + sb.ready, total * D * 3 * D * 2, 25e6, 0, "backward_input", 60,
    )
    sa.planes()
    sb.cores()
    token, (out, gi, gvec) = joined(token, sa.got[1:], [out, gi, gvec])
    gvec = gvec.reshape(links.depth, links.plane, 2, own, 128)
    gvec = pick(gvec, links.core, 2) + links.across_core(pick(gvec, 1 - links.core, 2))
    sb.cores_done(token, gvec)
    sb.planes()
    sa.planes_done(token)
    zero = jnp.zeros((), f32)
    sb.planes_done(zero)
    sb.ready = [jnp.concatenate([x, y], axis=-1) for x, y in zip(sa.ready, sb.ready)]
    sb.depths()
    sb.depths_done(zero)
    fa, fb = sb.result[:, : HALF + D], sb.result[:, HALF + D :]
    shard_up, shard_down = su.result, sd.result
    shard_qkv = jnp.concatenate(
        [f[:, k * HB : (k + 1) * HB] for k in range(3) for f in (fa, fb)], axis=1
    )
    shard_out = fa[:, HALF:]
    small = fb[:, HALF : HALF + UB + up_rows].T
    shard_up_shift = small[UB:].reshape(own_up)
    return (
        out,
        gi,
        small[GAIN1],
        small[SHIFT1],
        shard_qkv,
        small[QB],
        small[VB],
        shard_out,
        small[OB],
        small[GAIN2],
        small[SHIFT2],
        shard_up,
        shard_up_shift,
        shard_down,
        small[DB],
    )


def solution(mesh):
    rows = P("fsdp", None)
    cube = P("fsdp", None, None)
    one = P("fsdp")
    return jax.shard_map(
        functools.partial(on_device, mesh.shape["fsdp"]),
        mesh=mesh,
        in_specs=(cube, one, one, one, rows, one, one, rows, one, one, one, rows, one, rows, one, cube),
        out_specs=(cube, cube, one, one, rows, one, one, rows, one, one, one, rows, one, rows, one),
        check_vma=False,
    )
```
